512 devices in a mesh: len: 16 (over x_lo, y), height: 32 (over x_hi, z, core).
Axes of the slice: x: 4 (x_hi: 2, x_lo: 2; x = x_hi * 2 + x_lo), y: 8, z: 8, core: 2. Of those that a mesh axis runs over, the one named last changes fastest.
Arguments:
- position: float32 [3, 262144], P(None, ('len', 'height')), may hold values from -6 to 6
- velocity: float32 [3, 262144], P(None, ('len', 'height')), may hold values from -4 to 4
- tangent_pos: float32 [3, 32, 262144], P(None, None, ('len', 'height')), may hold values from -6 to 6
- tangent_vel: float32 [3, 32, 262144], P(None, None, ('len', 'height')), may hold values from -6 to 6
- mass: float32 [262144], P(('len', 'height')), may hold values from 0.5 to 2
- load_basis: float32 [3, 32, 262144], P(None, None, ('len', 'height')), may hold values from -2 to 2
- params: float32 [32], replicated, may hold values from -4 to 4
- stiffness: float32 [12, 262144], P(None, ('len', 'height')), may hold values from 0.5 to 2
- rest_length: float32 [12, 262144], P(None, ('len', 'height')), may hold values from 0.5 to 1.5
- neighbours: int32 [12, 262144], P(None, ('len', 'height')), may hold values from 0 to 1599, as said below
- intact: int32 [12, 262144], P(None, ('len', 'height')), may hold values 0 or 1
- face_lists: int32 [4, 131072], P(None, ('len', 'height')), may hold values from 0 to 511, as said below
- corner_lists: int32 [4, 8192], P(None, ('len', 'height')), may hold values from 0 to 511, as said below
- owned: int32 [512], P(('len', 'height')), may hold values from 256 to 512, as said below
Outputs:
- position_out: float32 [3, 262144], P(None, ('len', 'height'))
- velocity_out: float32 [3, 262144], P(None, ('len', 'height'))
- tangent_pos_out: float32 [3, 32, 262144], P(None, None, ('len', 'height'))
- tangent_vel_out: float32 [3, 32, 262144], P(None, None, ('len', 'height'))
The draws below stay inside these ranges and needn't reach their ends.
Inputs may be any that keep to these rules, and one draw needn't show every extreme that they name: `owned`: debris makes particle counts differ up to twofold between devices; at least one device is full. `neighbours`: an entry below 512 names a live particle of the same device; an entry 512 + f * 256 + g names row g of face block f, and an entry 1536 + c * 16 + g row g of diagonal block c; a ghost entry occurs only where the device it comes from exists. `face_lists`: every entry names a live particle of the sending device. `corner_lists`: every entry names a live particle of the sending device.
All inputs are finite; a program needn't handle non-finite values. No bound on the sum of `intact` on one device may be relied on, other than what follows from the above.
Results may differ from the reference program's by a relative error of at most 0.0001.
Values sent between devices are 32-bit elements; how exact they have to be, the bound alone decides.
No kernel may reach another device: no remote copies, remote signals or barrier semaphores. Data moves between devices by JAX's collectives and lax.ppermute only.
A program may use at most 64 MiB of HBM per device.

```python
import math
import jax
import jax.numpy as jnp
from jax import lax

P_DEV = 512
TANG = 32
BONDS = 12
STEPS = 2
GHOST = 256
CORNER = 16
STRIPS = 16
LEVELS = 32
PARTS_SIZE = 262144


def device_counts(key):
    first, second = jax.random.split(key)
    devices = STRIPS * LEVELS
    counts = jax.random.randint(first, (devices,), P_DEV // 2, P_DEV + 1)
    fullest = jax.random.randint(second, (), 0, devices)
    return jnp.where(jnp.arange(devices) == fullest, P_DEV, counts).astype(jnp.int32)


def draw_owned(key, part):
    counts = device_counts(key)
    return counts


def draw_neighbours(key, part):
    counts = device_counts(key)
    key = jax.random.fold_in(key, 11)
    keys = jax.random.split(key, 6)
    devices = STRIPS * LEVELS
    shape = (BONDS, devices, P_DEV)
    local = jax.random.randint(keys[0], shape, 0, 1 << 30) % counts[None, :, None]
    direction = jax.random.randint(keys[1], shape, 0, 4)
    face_slot = jax.random.randint(keys[2], shape, 0, GHOST)
    corner_slot = jax.random.randint(keys[4], shape, 0, CORNER)
    picked = jax.random.randint(keys[3], shape, 0, 10) < 4
    is_corner = jax.random.randint(keys[5], shape, 0, 16) == 0
    face_len = jnp.array([-1, 0, 0, 1], dtype=jnp.int32)
    face_up = jnp.array([0, -1, 1, 0], dtype=jnp.int32)
    corner_len = jnp.array([-1, -1, 1, 1], dtype=jnp.int32)
    corner_up = jnp.array([-1, 1, -1, 1], dtype=jnp.int32)
    side_len = jnp.where(is_corner, corner_len[direction], face_len[direction])
    side_up = jnp.where(is_corner, corner_up[direction], face_up[direction])
    device = jnp.arange(devices, dtype=jnp.int32)
    strip = (device // LEVELS)[None, :, None]
    level = (device % LEVELS)[None, :, None]
    source_len = strip - side_len
    source_up = level - side_up
    valid = (source_len >= 0) & (source_len < STRIPS) & (source_up >= 0) & (source_up < LEVELS)
    ghost = jnp.where(is_corner, P_DEV + 4 * GHOST + direction * CORNER + corner_slot, P_DEV + direction * GHOST + face_slot)
    value = jnp.where(picked & valid, ghost, local)
    corner = (device // LEVELS >= 1) & (device % LEVELS >= 1)
    value = value.at[0, :, 0].set(jnp.where(corner, P_DEV + 4 * GHOST + 4 * CORNER - 1, value[0, :, 0]))
    return value.reshape(BONDS, devices * P_DEV).astype(jnp.int32)


def draw_face_lists(key, part):
    counts = device_counts(key)
    key = jax.random.fold_in(key, 12)
    devices = STRIPS * LEVELS
    picks = jax.random.randint(key, (4, devices, GHOST), 0, 1 << 30) % counts[None, :, None]
    picks = picks.at[:, :, 0].set(jnp.broadcast_to(counts[None, :] - 1, (4, devices)))
    return picks.reshape(4, devices * GHOST).astype(jnp.int32)


def draw_corner_lists(key, part):
    counts = device_counts(key)
    key = jax.random.fold_in(key, 13)
    devices = STRIPS * LEVELS
    picks = jax.random.randint(key, (4, devices, CORNER), 0, 1 << 30) % counts[None, :, None]
    picks = picks.at[:, :, 0].set(jnp.broadcast_to(counts[None, :] - 1, (4, devices)))
    return picks.reshape(4, devices * CORNER).astype(jnp.int32)


def plant(values, key, low, high):
    extent = values.shape
    place = [jax.random.randint(jax.random.fold_in(key, axis), (), 0, extent[axis]) for axis in range(len(extent))]
    values = values.at[tuple(place)].set(low)
    longest = extent.index(max(extent))
    place[longest] = (place[longest] + 1) % extent[longest]
    return values.at[tuple(place)].set(high)


def shard_levels(key, dims, pieces, least, high):
    factor_of, own = 1.0, jax.random.fold_in(key, 6)
    for dim, shards_of in pieces:
        steps = jnp.exp(jax.random.uniform(jax.random.fold_in(own, dim), (shards_of,), jnp.float32, least / len(pieces), high / len(pieces)))
        factor_of = factor_of * jnp.repeat(steps, dims[dim] // shards_of).reshape([-1 if axis == dim else 1 for axis in range(len(dims))])
    return factor_of


def centred(key, dims, deviation, limit, pieces=(), kind=jnp.bfloat16):
    loudness = shard_levels(key, dims, pieces, -0.22, 0.18) if pieces else 1.0
    values = jax.random.normal(key, dims, jnp.float32) * deviation * loudness
    return jnp.minimum(jnp.maximum(values, -limit), limit).astype(kind)


def setup_inputs(seed: int = 0) -> dict:
    splits = jax.random.split(jax.random.key(seed), 15)
    position = centred(splits[0], (3, PARTS_SIZE), 1.0, 6.0, ((1, 512),), jnp.float32)
    velocity = centred(splits[1], (3, PARTS_SIZE), 0.5, 4.0, ((1, 512),), jnp.float32)
    tangent_pos = centred(splits[2], (3, TANG, PARTS_SIZE), 1.0, 6.0, ((2, 512),), jnp.float32)
    tangent_vel = centred(splits[3], (3, TANG, PARTS_SIZE), 1.0, 6.0, ((2, 512),), jnp.float32)
    mass = jnp.clip(jnp.exp(math.log(2.0) - 1.3862944 * jax.random.uniform(splits[4], (PARTS_SIZE,), jnp.float32) ** shard_levels(splits[4], (PARTS_SIZE,), ((0, 512),), -0.2, 0.2)), 0.5, 2.0)
    load_basis = centred(splits[5], (3, TANG, PARTS_SIZE), 0.3, 2.0, ((2, 512),), jnp.float32)
    params = centred(splits[6], (TANG,), 1.0, 4.0, (), jnp.float32)
    stiffness = jnp.clip(jnp.exp(math.log(2.0) - 1.3862944 * jax.random.uniform(splits[7], (BONDS, PARTS_SIZE), jnp.float32) ** shard_levels(splits[7], (BONDS, PARTS_SIZE), ((1, 512),), -0.2, 0.2)), 0.5, 2.0)
    rest_length = jnp.clip(0.5 + 1.0 * jax.random.uniform(splits[8], (BONDS, PARTS_SIZE), jnp.float32) ** shard_levels(splits[8], (BONDS, PARTS_SIZE), ((1, 512),), -0.2, 0.2), 0.5, 1.5)
    neighbours = draw_neighbours(jax.random.fold_in(splits[14], 71), 0)
    intact = plant((jax.random.randint(splits[10], (BONDS, PARTS_SIZE), 0, 10) < 9).astype(jnp.int32), jax.random.fold_in(splits[10], 1), 0, 1)
    face_lists = draw_face_lists(jax.random.fold_in(splits[14], 71), 0)
    corner_lists = draw_corner_lists(jax.random.fold_in(splits[14], 71), 0)
    owned = draw_owned(jax.random.fold_in(splits[14], 71), 0)
    return {"position": position, "velocity": velocity, "tangent_pos": tangent_pos, "tangent_vel": tangent_vel, "mass": mass, "load_basis": load_basis, "params": params, "stiffness": stiffness, "rest_length": rest_length, "neighbours": neighbours, "intact": intact, "face_lists": face_lists, "corner_lists": corner_lists, "owned": owned}


face_dirs = ((-1, 0), (0, -1), (0, 1), (1, 0))
corner_dirs = ((-1, -1), (-1, 1), (1, -1), (1, 1))

def bond_sum(table, index_rows, weight_rows, state, stiffness, rest_length, totals):
    force, dforce = totals
    for bond in range(index_rows.shape[0]):
        rows = jnp.take(table, index_rows[bond], axis=2)
        delta = rows[:, 0, :] - state[:, 0, :]
        dtang = rows[:, 1:, :] - state[:, 1:, :]
        radius = jnp.sqrt(lax.optimization_barrier(jnp.sum(delta * delta, axis=0)) + 0.25)
        scaled = stiffness[bond] * (1.0 - rest_length[bond] / radius)
        curved = stiffness[bond] * rest_length[bond] / (radius * radius * radius)
        along_dir = lax.optimization_barrier(jnp.sum(delta[:, None, :] * dtang, axis=0))
        force = force + weight_rows[bond] * scaled * delta
        dforce = dforce + weight_rows[bond] * (scaled * dtang + (curved * along_dir)[None] * delta[:, None, :])
    return (force, dforce)

def reference(position, velocity, tangent_pos, tangent_vel, mass, load_basis, params, stiffness, rest_length, neighbours, intact, face_lists, corner_lists, owned):
    devices = STRIPS * LEVELS

    def split_dev(array):
        shaped = array.reshape(array.shape[:-1] + (devices, array.shape[-1] // devices))
        return jnp.moveaxis(shaped, -2, 0)

    def join_dev(array):
        moved = jnp.moveaxis(array, 0, -2)
        return moved.reshape(moved.shape[:-2] + (devices * moved.shape[-1],))
    pos = split_dev(position)
    vel = split_dev(velocity)
    tpos = split_dev(tangent_pos)
    tvel = split_dev(tangent_vel)
    masses = split_dev(mass)
    basis = split_dev(load_basis)
    stiff = split_dev(stiffness)
    rests = split_dev(rest_length)
    partner = split_dev(neighbours)
    faces_dev = split_dev(face_lists)
    corners_dev = split_dev(corner_lists)
    live = (jnp.arange(P_DEV, dtype=jnp.int32)[None, :] < owned[:, None]).astype(jnp.float32)
    weights = split_dev(intact).astype(jnp.float32) * live[:, None, :]
    external = jnp.einsum('dcpn,p->dcn', basis, params, precision=lax.Precision.HIGHEST)

    def sender(state_one, list_one):
        return jnp.stack([jnp.take(state_one, list_one[index], axis=2) for index in range(4)])

    def local_forces(table, index_rows, weight_rows, state_one, stiff_one, rest_one):
        zeros = (jnp.zeros((3, P_DEV), jnp.float32), jnp.zeros((3, TANG, P_DEV), jnp.float32))
        return bond_sum(table, index_rows, weight_rows, state_one, stiff_one, rest_one, zeros)

    def arrive(sent, width, dirs):
        grid = sent.reshape(STRIPS, LEVELS, 4, 3, TANG + 1, width)
        padded = jnp.pad(grid, ((1, 1), (1, 1), (0, 0), (0, 0), (0, 0), (0, 0)))
        blocks = []
        for index, pair in enumerate(dirs):
            blocks.append(padded[1 - pair[0]:1 - pair[0] + STRIPS, 1 - pair[1]:1 - pair[1] + LEVELS, index])
        return jnp.concatenate(blocks, axis=-1).reshape(devices, 3, TANG + 1, 4 * width)
    for step in range(STEPS):
        state = jnp.concatenate([pos[:, :, None, :], tpos], axis=2)
        face_rows = arrive(jax.vmap(sender)(state, faces_dev), GHOST, face_dirs)
        corner_rows = arrive(jax.vmap(sender)(state, corners_dev), CORNER, corner_dirs)
        table = jnp.concatenate([state, face_rows, corner_rows], axis=-1)
        force, dforce = jax.vmap(local_forces)(table, partner, weights, state, stiff, rests)
        vel = vel + 0.05 * ((force + external) / masses[:, None, :])
        pos = pos + 0.05 * vel
        tvel = tvel + 0.05 * ((dforce + basis) / masses[:, None, None, :])
        tpos = tpos + 0.05 * tvel
    return (join_dev(pos), join_dev(vel), join_dev(tpos), join_dev(tvel))
```

```python
import jax
import jax.numpy as jnp
from jax import lax
from jax.experimental import pallas as pl
from jax.experimental.pallas import tpu as pltpu
from jax.sharding import PartitionSpec as P

STEPS = 2
DT = 0.05
FACE = 256
CORNER = 16
MESSAGE = FACE + 128
ROWS = 104
AXES = ("len", "height")
PARAMS = pltpu.CompilerParams(vmem_limit_bytes=16 * 2**20)


def matching(strips, levels, along, odd):
    pairs = []
    for l in range(strips):
        for h in range(levels):
            place, size = (l, strips) if along == 0 else (h, levels)
            other = place + 1 if place % 2 == odd else place - 1
            if 0 <= other < size:
                pairs.append((l * levels + h, other * levels + h if along == 0 else l * levels + other))
    return pairs


def halves(table):
    high = table.astype(jnp.bfloat16).astype(jnp.float32)
    return jnp.concatenate([high, table - high], axis=0).astype(jnp.bfloat16)


def one_hot(index, rows):
    lanes = index.shape[1]
    wanted = jnp.broadcast_to(index, (16, lanes)).astype(jnp.int16)
    base = lax.broadcasted_iota(jnp.int16, (16, lanes), 0)
    one = jnp.ones((16, lanes), jnp.bfloat16)
    zero = jnp.zeros((16, lanes), jnp.bfloat16)
    parts = [jnp.where(wanted == base + jnp.int16(first), one, zero) for first in range(0, rows, 16)]
    return jnp.concatenate(parts, axis=0)


def pick(table, index):
    both = jnp.dot(table, one_hot(index, table.shape[1]), preferred_element_type=jnp.float32)
    return both[:ROWS] + both[ROWS:]


def stacked(tangent, position):
    lanes = position.shape[1]
    tang = tangent.shape[0] * tangent.shape[1]
    flat = tangent.reshape(tang, lanes)
    return jnp.concatenate([flat, position, jnp.zeros((ROWS - tang - 3, lanes), jnp.float32)], axis=0)


def pack(table, sends, first, second, third, fourth):
    first[...] = pick(table, sends[0:1, :])
    second[...] = pick(table, sends[1:2, :])
    third[...] = pick(table, sends[2:3, :FACE])
    fourth[...] = pick(table, sends[3:4, :FACE])


def bonds_into(total, table, index, inside, tangent, position, stiffness, rest_length, intact, owned):
    count = position.shape[1]
    tang = tangent.shape[1]
    slot = lax.broadcasted_iota(jnp.int32, (1, count), 1)
    live = slot < owned
    own = [tangent[c] for c in range(3)]
    force = [total[3 * tang + c : 3 * tang + c + 1, :] for c in range(3)]
    for bond in range(index.shape[0]):
        rows = pick(table, index[bond : bond + 1, :])
        weight = jnp.where(live & inside[bond : bond + 1, :], intact[bond : bond + 1, :].astype(jnp.float32), 0.0)
        stiff = stiffness[bond : bond + 1, :] * weight
        rest = rest_length[bond : bond + 1, :]
        delta = [rows[3 * tang + c : 3 * tang + c + 1, :] - position[c : c + 1, :] for c in range(3)]
        inverse = lax.rsqrt(delta[0] * delta[0] + delta[1] * delta[1] + delta[2] * delta[2] + 0.25)
        scaled = stiff * (1.0 - rest * inverse)
        curved = stiff * rest * (inverse * inverse * inverse)
        dtang = [rows[c * tang : (c + 1) * tang, :] - own[c] for c in range(3)]
        along = delta[0] * dtang[0] + delta[1] * dtang[1] + delta[2] * dtang[2]
        for c in range(3):
            force[c] = force[c] + scaled * delta[c]
            total[c * tang : (c + 1) * tang, :] += scaled * dtang[c] + (curved * delta[c]) * along
    for c in range(3):
        total[3 * tang + c : 3 * tang + c + 1, :] = force[c]


def place_of(index, odd):
    own = index < 512
    face = (index - 512) >> 8
    is_corner = index >= 1536
    corner = (index - 1536) >> 4
    upward = jnp.where(is_corner, corner & 1, (face >> 1) & 1)
    forward = jnp.where(is_corner, corner >> 1, (face >> 1) & 1)
    second_l = jnp.where(forward == odd[0], 1, 0)
    second_h = jnp.where(upward == odd[1], 1, 0)
    on_l = (face == 0) | (face == 3)
    at_face = jnp.where(on_l, 512 + 256 * second_l, 1024 + 256 * second_h) + (index & 255)
    at_corner = 1536 + 32 * second_h + 16 * second_l + (index & 15)
    return jnp.where(own, index, jnp.where(is_corner, at_corner, at_face))


def pack_kernel(tangent, position, sends, first, second, third, fourth):
    table = halves(stacked(tangent[...], position[...]))
    pack(table, sends, first, second, third, fourth)


def own_kernel(odd, owned, params, tangent, position, basis, stiffness, rest_length, neighbours, intact, total):
    tang = tangent.shape[1]
    count = position.shape[1]
    for c in range(3):
        total[c * tang : (c + 1) * tang, :] = basis[c]
        outer = jnp.zeros((1, count), jnp.float32)
        for p in range(tang):
            outer = outer + params[p] * basis[c, p : p + 1, :]
        total[3 * tang + c : 3 * tang + c + 1, :] = outer
    total[3 * tang + 3 : ROWS, :] = jnp.zeros((ROWS - 3 * tang - 3, count), jnp.float32)
    table = halves(stacked(tangent[...], position[...]))
    index = neighbours[...]
    inside = index < 512
    bonds_into(total, table, index, inside, tangent, position, stiffness, rest_length, intact, owned[0])


def len_kernel(odd, owned, before, first, second, tangent, position, stiffness, rest_length, neighbours, intact, total):
    total[...] = before[...]
    table = halves(jnp.concatenate([first[:, :FACE], second[:, :FACE]], axis=1))
    index = place_of(neighbours[...], odd) - 512
    inside = (index >= 0) & (index < 512)
    bonds_into(total, table, index, inside, tangent, position, stiffness, rest_length, intact, owned[0])


def height_kernel(last):
    def body(odd, owned, before, third, fourth, tangent, position, tangent_vel, velocity, mass, stiffness, rest_length, neighbours, intact, sends, *outs):
        new_tangent, new_position, new_tangent_vel, new_velocity = outs[:4]
        total = outs[-1]
        tang = tangent.shape[1]
        total[...] = before[...]
        lane = lax.broadcasted_iota(jnp.int32, (ROWS, 128), 1)
        corners = jnp.where(lane < 32, third[:, FACE:], fourth[:, FACE:])
        table = halves(jnp.concatenate([third[:, :FACE], fourth[:, :FACE], corners], axis=1))
        index = place_of(neighbours[...], odd) - 1024
        inside = index >= 0
        bonds_into(total, table, index, inside, tangent, position, stiffness, rest_length, intact, owned[0])
        pace = DT / mass[...]
        for c in range(3):
            speed = tangent_vel[c] + pace * total[c * tang : (c + 1) * tang, :]
            new_tangent_vel[c] = speed
            new_tangent[c] = tangent[c] + DT * speed
        speed = velocity[...] + pace * total[3 * tang : 3 * tang + 3, :]
        new_velocity[...] = speed
        new_position[...] = position[...] + DT * speed
        if not last:
            table = halves(stacked(new_tangent[...], new_position[...]))
            pack(table, sends, *outs[4:8])

    return body


def cost(columns, bonds, moved):
    return pl.CostEstimate(flops=2 * 2 * ROWS * columns * bonds * 512, bytes_accessed=moved, transcendentals=0)


def f32(*shape):
    return jax.ShapeDtypeStruct(shape, jnp.float32)


VMEM = pl.BlockSpec(memory_space=pltpu.VMEM)
SMEM = pl.BlockSpec(memory_space=pltpu.SMEM)


def on_device(
    position,
    velocity,
    tangent_pos,
    tangent_vel,
    mass,
    load_basis,
    params,
    stiffness,
    rest_length,
    neighbours,
    intact,
    face_lists,
    corner_lists,
    owned,
):
    count = position.shape[1]
    bonds = neighbours.shape[0]
    strips, levels = lax.axis_size("len"), lax.axis_size("height")
    odd_l = lax.axis_index("len") % 2
    odd_h = lax.axis_index("height") % 2
    odd = jnp.stack([odd_l, odd_h]).astype(jnp.int32)
    mass = mass.reshape(1, count)

    def either(flag, yes, no):
        return jnp.where(flag == 1, yes, no)

    blank = jnp.full((CORNER,), -1, jnp.int32)
    rest_blank = jnp.full((64,), -1, jnp.int32)
    up = [either(odd_h, corner_lists[2 * a + 1], corner_lists[2 * a]) for a in range(2)]
    down = [either(odd_h, corner_lists[2 * a], corner_lists[2 * a + 1]) for a in range(2)]
    sends = jnp.stack(
        [
            jnp.concatenate([either(odd_l, face_lists[3], face_lists[0]), either(odd_l, up[1], up[0]), blank, either(odd_l, down[1], down[0]), blank, rest_blank]),
            jnp.concatenate([either(odd_l, face_lists[0], face_lists[3]), blank, either(odd_l, up[0], up[1]), blank, either(odd_l, down[0], down[1]), rest_blank]),
            jnp.concatenate([either(odd_h, face_lists[2], face_lists[1]), blank, blank, blank, blank, rest_blank]),
            jnp.concatenate([either(odd_h, face_lists[1], face_lists[2]), blank, blank, blank, blank, rest_blank]),
        ]
    )
    packed = (f32(ROWS, MESSAGE), f32(ROWS, MESSAGE), f32(ROWS, FACE), f32(ROWS, FACE))
    messages = pl.pallas_call(
        pack_kernel,
        out_shape=packed,
        compiler_params=PARAMS,
        cost_estimate=cost(512, 3, 700000),
        name="pack",
    )(tangent_pos, position, sends)
    for step in range(STEPS):
        last = step == STEPS - 1
        first = lax.ppermute(messages[0], AXES, matching(strips, levels, 0, 1))
        second = lax.ppermute(messages[1], AXES, matching(strips, levels, 0, 0))
        total = pl.pallas_call(
            own_kernel,
            out_shape=f32(ROWS, count),
            in_specs=[SMEM] * 3 + [VMEM] * 7,
            compiler_params=PARAMS,
            cost_estimate=cost(512, bonds, 1000000),
            name="own_bonds",
        )(odd, owned, params, tangent_pos, position, load_basis, stiffness, rest_length, neighbours, intact)
        corners = first[:, FACE:] + second[:, FACE:]
        third = lax.ppermute(jnp.concatenate([messages[2], corners], axis=1), AXES, matching(strips, levels, 1, 1))
        fourth = lax.ppermute(jnp.concatenate([messages[3], corners], axis=1), AXES, matching(strips, levels, 1, 0))
        total = pl.pallas_call(
            len_kernel,
            out_shape=f32(ROWS, count),
            in_specs=[SMEM] * 2 + [VMEM] * 9,
            compiler_params=PARAMS,
            cost_estimate=cost(512, bonds, 1000000),
            name="len_bonds",
        )(odd, owned, total, first, second, tangent_pos, position, stiffness, rest_length, neighbours, intact)
        state = (f32(*tangent_pos.shape), f32(*position.shape), f32(*tangent_pos.shape), f32(*position.shape))
        out = pl.pallas_call(
            height_kernel(last),
            out_shape=state if last else state + packed,
            in_specs=[SMEM] * 2 + [VMEM] * 13,
            scratch_shapes=[pltpu.VMEM((ROWS, count), jnp.float32)],
            compiler_params=PARAMS,
            cost_estimate=cost(640, bonds, 1500000),
            name="height_bonds",
        )(odd, owned, total, third, fourth, tangent_pos, position, tangent_vel, velocity, mass, stiffness, rest_length, neighbours, intact, sends)
        tangent_pos, position, tangent_vel, velocity = out[:4]
        messages = out[4:]
    return (position, velocity, tangent_pos, tangent_vel)


def solution(mesh):
    placed = (
        P(None, ("len", "height")),
        P(None, ("len", "height")),
        P(None, None, ("len", "height")),
        P(None, None, ("len", "height")),
        P(("len", "height")),
        P(None, None, ("len", "height")),
        P(),
        P(None, ("len", "height")),
        P(None, ("len", "height")),
        P(None, ("len", "height")),
        P(None, ("len", "height")),
        P(None, ("len", "height")),
        P(None, ("len", "height")),
        P(("len", "height")),
    )
    return jax.shard_map(
        on_device,
        mesh=mesh,
        in_specs=placed,
        out_specs=(
            P(None, ("len", "height")),
            P(None, ("len", "height")),
            P(None, None, ("len", "height")),
            P(None, None, ("len", "height")),
        ),
        check_vma=False,
    )
```

```python
import jax
import jax.numpy as jnp
from jax import lax
from jax.experimental import pallas as pl
from jax.experimental.pallas import tpu as pltpu
from jax.sharding import PartitionSpec as P

STEPS = 2
DT = 0.05
FACE = 256
CORNER = 16
ROWS = 104
MESSAGE = ROWS + 16
GROUPS = ROWS // 8
AXES = ("len", "height")
PARAMS = pltpu.CompilerParams(vmem_limit_bytes=16 * 2**20)


def matching(strips, levels, along, odd):
    pairs = []
    for l in range(strips):
        for h in range(levels):
            place, size = (l, strips) if along == 0 else (h, levels)
            other = place + 1 if place % 2 == odd else place - 1
            if 0 <= other < size:
                pairs.append((l * levels + h, other * levels + h if along == 0 else l * levels + other))
    return pairs


def halves(table):
    high = table.astype(jnp.bfloat16).astype(jnp.float32)
    return jnp.concatenate([high, table - high], axis=0).astype(jnp.bfloat16)


def one_hot(index, rows):
    lanes = index.shape[1]
    wanted = jnp.broadcast_to(index, (16, lanes)).astype(jnp.int16)
    base = lax.broadcasted_iota(jnp.int16, (16, lanes), 0)
    one = jnp.ones((16, lanes), jnp.bfloat16)
    zero = jnp.zeros((16, lanes), jnp.bfloat16)
    parts = [jnp.where(wanted == base + jnp.int16(first), one, zero) for first in range(0, rows, 16)]
    return jnp.concatenate(parts, axis=0)


def pick(table, index):
    both = jnp.dot(table, one_hot(index, table.shape[1]), preferred_element_type=jnp.float32)
    return both[:ROWS] + both[ROWS:]


def stacked(tangent, position):
    lanes = position.shape[1]
    tang = tangent.shape[0] * tangent.shape[1]
    flat = tangent.reshape(tang, lanes)
    return jnp.concatenate([flat, position, jnp.zeros((ROWS - tang - 3, lanes), jnp.float32)], axis=0)


def fold(columns):
    slot = lax.broadcasted_iota(jnp.int32, (8, FACE), 1) >> 5
    parts = []
    for first in range(0, GROUPS, 8):
        part = jnp.zeros((8, FACE), jnp.float32)
        for group in range(first, min(first + 8, GROUPS)):
            part = jnp.where(slot == group - first, columns[8 * group : 8 * group + 8, :], part)
        parts.append(part)
    return jnp.concatenate(parts, axis=0)


def unfold(one, two):
    lane = lax.broadcasted_iota(jnp.int32, (16, 128), 1)
    moved = []
    for slot in range(8):
        back = (FACE - 32 * slot) % FACE
        left = one if back == 0 else pltpu.roll(one, back, 1)
        right = pltpu.roll(two, (back + 32) % FACE, 1) if (back + 32) % FACE else two
        moved.append(jnp.where(lane < 32, left[:, :128], right[:, :128]))
    parts = [moved[group % 8][8 * (group // 8) : 8 * (group // 8) + 8, :] for group in range(GROUPS)]
    return jnp.concatenate(parts, axis=0)


def pack(table, sends, first, second, third, fourth):
    first[:ROWS, :] = pick(table, sends[0:1, :])
    first[ROWS:, :] = fold(pick(table, sends[4:5, :]))
    second[:ROWS, :] = pick(table, sends[1:2, :])
    second[ROWS:, :] = fold(pick(table, sends[5:6, :]))
    third[...] = pick(table, sends[2:3, :])
    fourth[...] = pick(table, sends[3:4, :])


def bonds_into(total, table, index, inside, tangent, position, stiffness, rest_length, intact, owned):
    count = position.shape[1]
    tang = tangent.shape[1]
    slot = lax.broadcasted_iota(jnp.int32, (1, count), 1)
    live = slot < owned
    own = [tangent[c] for c in range(3)]
    force = [total[3 * tang + c : 3 * tang + c + 1, :] for c in range(3)]
    for bond in range(index.shape[0]):
        rows = pick(table, index[bond : bond + 1, :])
        weight = jnp.where(live & inside[bond : bond + 1, :], intact[bond : bond + 1, :].astype(jnp.float32), 0.0)
        stiff = stiffness[bond : bond + 1, :] * weight
        rest = rest_length[bond : bond + 1, :]
        delta = [rows[3 * tang + c : 3 * tang + c + 1, :] - position[c : c + 1, :] for c in range(3)]
        inverse = lax.rsqrt(delta[0] * delta[0] + delta[1] * delta[1] + delta[2] * delta[2] + 0.25)
        scaled = stiff * (1.0 - rest * inverse)
        curved = stiff * rest * (inverse * inverse * inverse)
        dtang = [rows[c * tang : (c + 1) * tang, :] - own[c] for c in range(3)]
        along = delta[0] * dtang[0] + delta[1] * dtang[1] + delta[2] * dtang[2]
        for c in range(3):
            force[c] = force[c] + scaled * delta[c]
            total[c * tang : (c + 1) * tang, :] += scaled * dtang[c] + (curved * delta[c]) * along
    for c in range(3):
        total[3 * tang + c : 3 * tang + c + 1, :] = force[c]


def place_of(index, odd):
    own = index < 512
    face = (index - 512) >> 8
    is_corner = index >= 1536
    corner = (index - 1536) >> 4
    upward = jnp.where(is_corner, corner & 1, (face >> 1) & 1)
    forward = jnp.where(is_corner, corner >> 1, (face >> 1) & 1)
    second_l = jnp.where(forward == odd[0], 1, 0)
    second_h = jnp.where(upward == odd[1], 1, 0)
    on_l = (face == 0) | (face == 3)
    at_face = jnp.where(on_l, 512 + 256 * second_l, 1280 - 256 * second_h) + (index & 255)
    at_corner = 1536 + 32 * second_h + 16 * (second_l ^ second_h) + (index & 15)
    return jnp.where(own, index, jnp.where(is_corner, at_corner, at_face))


def pack_kernel(tangent, position, sends, first, second, third, fourth):
    table = halves(stacked(tangent[...], position[...]))
    pack(table, sends, first, second, third, fourth)


def own_kernel(odd, owned, params, tangent, position, basis, stiffness, rest_length, neighbours, intact, total):
    tang = tangent.shape[1]
    count = position.shape[1]
    for c in range(3):
        total[c * tang : (c + 1) * tang, :] = basis[c]
        outer = jnp.zeros((1, count), jnp.float32)
        for p in range(tang):
            outer = outer + params[p] * basis[c, p : p + 1, :]
        total[3 * tang + c : 3 * tang + c + 1, :] = outer
    total[3 * tang + 3 : ROWS, :] = jnp.zeros((ROWS - 3 * tang - 3, count), jnp.float32)
    table = halves(stacked(tangent[...], position[...]))
    index = neighbours[...]
    inside = index < 512
    bonds_into(total, table, index, inside, tangent, position, stiffness, rest_length, intact, owned[0])


def side_kernel(odd, owned, before, first, second, fourth, tangent, position, stiffness, rest_length, neighbours, intact, total):
    total[...] = before[...]
    table = halves(jnp.concatenate([first[:ROWS, :], second[:ROWS, :], fourth[:ROWS, :]], axis=1))
    index = place_of(neighbours[...], odd) - 512
    inside = (index >= 0) & (index < 768)
    bonds_into(total, table, index, inside, tangent, position, stiffness, rest_length, intact, owned[0])


def height_kernel(last):
    def body(odd, owned, before, third, fourth, tangent, position, tangent_vel, velocity, mass, stiffness, rest_length, neighbours, intact, sends, *outs):
        new_tangent, new_position, new_tangent_vel, new_velocity = outs[:4]
        total = outs[-1]
        tang = tangent.shape[1]
        total[...] = before[...]
        corners = unfold(third[ROWS:, :], fourth[ROWS:, :])
        table = halves(jnp.concatenate([third[:ROWS, :], corners], axis=1))[:, : FACE + 64]
        index = place_of(neighbours[...], odd) - 1280
        inside = index >= 0
        bonds_into(total, table, index, inside, tangent, position, stiffness, rest_length, intact, owned[0])
        pace = DT / mass[...]
        for c in range(3):
            speed = tangent_vel[c] + pace * total[c * tang : (c + 1) * tang, :]
            new_tangent_vel[c] = speed
            new_tangent[c] = tangent[c] + DT * speed
        speed = velocity[...] + pace * total[3 * tang : 3 * tang + 3, :]
        new_velocity[...] = speed
        new_position[...] = position[...] + DT * speed
        if not last:
            table = halves(stacked(new_tangent[...], new_position[...]))
            pack(table, sends, *outs[4:8])

    return body


def cost(columns, bonds, moved):
    return pl.CostEstimate(flops=2 * 2 * ROWS * columns * bonds * 512, bytes_accessed=moved, transcendentals=0)


def f32(*shape):
    return jax.ShapeDtypeStruct(shape, jnp.float32)


VMEM = pl.BlockSpec(memory_space=pltpu.VMEM)
SMEM = pl.BlockSpec(memory_space=pltpu.SMEM)


def on_device(
    position,
    velocity,
    tangent_pos,
    tangent_vel,
    mass,
    load_basis,
    params,
    stiffness,
    rest_length,
    neighbours,
    intact,
    face_lists,
    corner_lists,
    owned,
):
    count = position.shape[1]
    bonds = neighbours.shape[0]
    strips, levels = lax.axis_size("len"), lax.axis_size("height")
    odd_l = lax.axis_index("len") % 2
    odd_h = lax.axis_index("height") % 2
    odd = jnp.stack([odd_l, odd_h]).astype(jnp.int32)
    mass = mass.reshape(1, count)

    def either(flag, yes, no):
        return jnp.where(flag == 1, yes, no)

    up = [either(odd_h, corner_lists[2 * a + 1], corner_lists[2 * a]) for a in range(2)]
    down = [either(odd_h, corner_lists[2 * a], corner_lists[2 * a + 1]) for a in range(2)]
    sends = jnp.stack(
        [
            either(odd_l, face_lists[3], face_lists[0]),
            either(odd_l, face_lists[0], face_lists[3]),
            either(odd_h, face_lists[2], face_lists[1]),
            either(odd_h, face_lists[1], face_lists[2]),
            jnp.tile(jnp.concatenate([either(odd_l, up[1], up[0]), either(odd_l, down[1], down[0])]), 8),
            jnp.tile(jnp.concatenate([either(odd_l, down[0], down[1]), either(odd_l, up[0], up[1])]), 8),
        ]
    )
    low = lax.broadcasted_iota(jnp.int32, (MESSAGE - ROWS, FACE), 1) % 32 < CORNER
    packed = (f32(MESSAGE, FACE), f32(MESSAGE, FACE), f32(ROWS, FACE), f32(ROWS, FACE))
    messages = pl.pallas_call(
        pack_kernel,
        out_shape=packed,
        compiler_params=PARAMS,
        cost_estimate=cost(512, 3, 700000),
        name="pack",
    )(tangent_pos, position, sends)
    for step in range(STEPS):
        last = step == STEPS - 1
        first = lax.ppermute(messages[0], AXES, matching(strips, levels, 0, 1))
        second = lax.ppermute(messages[1], AXES, matching(strips, levels, 0, 0))
        total = pl.pallas_call(
            own_kernel,
            out_shape=f32(ROWS, count),
            in_specs=[SMEM] * 3 + [VMEM] * 7,
            compiler_params=PARAMS,
            cost_estimate=cost(512, bonds, 1000000),
            name="own_bonds",
        )(odd, owned, params, tangent_pos, position, load_basis, stiffness, rest_length, neighbours, intact)
        first, second, total = lax.optimization_barrier((first, second, total))
        mine = jnp.where(low, second[ROWS:], first[ROWS:])
        fourth = lax.ppermute(jnp.concatenate([messages[3], mine]), AXES, matching(strips, levels, 1, 0))
        mine = jnp.where(low, first[ROWS:], second[ROWS:])
        third = lax.ppermute(jnp.concatenate([messages[2], mine]), AXES, matching(strips, levels, 1, 1))
        total = pl.pallas_call(
            side_kernel,
            out_shape=f32(ROWS, count),
            in_specs=[SMEM] * 2 + [VMEM] * 10,
            compiler_params=PARAMS,
            cost_estimate=cost(768, bonds, 1000000),
            name="side_bonds",
        )(odd, owned, total, first, second, fourth, tangent_pos, position, stiffness, rest_length, neighbours, intact)
        state = (f32(*tangent_pos.shape), f32(*position.shape), f32(*tangent_pos.shape), f32(*position.shape))
        out = pl.pallas_call(
            height_kernel(last),
            out_shape=state if last else state + packed,
            in_specs=[SMEM] * 2 + [VMEM] * 13,
            scratch_shapes=[pltpu.VMEM((ROWS, count), jnp.float32)],
            compiler_params=PARAMS,
            cost_estimate=cost(320, bonds, 1500000),
            name="height_bonds",
        )(odd, owned, total, third, fourth, tangent_pos, position, tangent_vel, velocity, mass, stiffness, rest_length, neighbours, intact, sends)
        tangent_pos, position, tangent_vel, velocity = out[:4]
        messages = out[4:]
    return (position, velocity, tangent_pos, tangent_vel)


def solution(mesh):
    placed = (
        P(None, ("len", "height")),
        P(None, ("len", "height")),
        P(None, None, ("len", "height")),
        P(None, None, ("len", "height")),
        P(("len", "height")),
        P(None, None, ("len", "height")),
        P(),
        P(None, ("len", "height")),
        P(None, ("len", "height")),
        P(None, ("len", "height")),
        P(None, ("len", "height")),
        P(None, ("len", "height")),
        P(None, ("len", "height")),
        P(("len", "height")),
    )
    return jax.shard_map(
        on_device,
        mesh=mesh,
        in_specs=placed,
        out_specs=(
            P(None, ("len", "height")),
            P(None, ("len", "height")),
            P(None, None, ("len", "height")),
            P(None, None, ("len", "height")),
        ),
        check_vma=False,
    )
```

```python
import jax
import jax.numpy as jnp
from jax import lax
from jax.experimental import pallas as pl
from jax.experimental.pallas import tpu as pltpu
from jax.sharding import PartitionSpec as P

STEPS = 2
DT = 0.05
FACE = 256
CORNER = 16
ROWS = 104
MESSAGE = ROWS + 16
GROUPS = ROWS // 8
AXES = ("len", "height")
PARAMS = pltpu.CompilerParams(vmem_limit_bytes=16 * 2**20)


def matching(strips, levels, along, odd):
    pairs = []
    for l in range(strips):
        for h in range(levels):
            place, size = (l, strips) if along == 0 else (h, levels)
            other = place + 1 if place % 2 == odd else place - 1
            if 0 <= other < size:
                pairs.append((l * levels + h, other * levels + h if along == 0 else l * levels + other))
    return pairs


def couples(strips, levels):
    return [[l * levels + h, l * levels + h + 1] for l in range(strips) for h in range(0, levels, 2)]


def halves(table):
    high = table.astype(jnp.bfloat16).astype(jnp.float32)
    return jnp.concatenate([high, table - high], axis=0).astype(jnp.bfloat16)


def one_hot(index, rows):
    lanes = index.shape[1]
    wanted = jnp.broadcast_to(index, (16, lanes)).astype(jnp.int16)
    base = lax.broadcasted_iota(jnp.int16, (16, lanes), 0)
    one = jnp.ones((16, lanes), jnp.bfloat16)
    zero = jnp.zeros((16, lanes), jnp.bfloat16)
    parts = [jnp.where(wanted == base + jnp.int16(first), one, zero) for first in range(0, rows, 16)]
    return jnp.concatenate(parts, axis=0)


def pick(table, index):
    both = jnp.dot(table, one_hot(index, table.shape[1]), preferred_element_type=jnp.float32)
    return both[:ROWS] + both[ROWS:]


def stacked(tangent, position):
    lanes = position.shape[1]
    tang = tangent.shape[0] * tangent.shape[1]
    flat = tangent.reshape(tang, lanes)
    return jnp.concatenate([flat, position, jnp.zeros((ROWS - tang - 3, lanes), jnp.float32)], axis=0)


def fold(columns):
    slot = lax.broadcasted_iota(jnp.int32, (8, FACE), 1) >> 5
    parts = []
    for first in range(0, GROUPS, 8):
        part = jnp.zeros((8, FACE), jnp.float32)
        for group in range(first, min(first + 8, GROUPS)):
            part = jnp.where(slot == group - first, columns[8 * group : 8 * group + 8, :], part)
        parts.append(part)
    return jnp.concatenate(parts, axis=0)


def unfold(one, two):
    lane = lax.broadcasted_iota(jnp.int32, (16, 128), 1)
    moved = []
    for slot in range(8):
        back = (FACE - 32 * slot) % FACE
        left = one if back == 0 else pltpu.roll(one, back, 1)
        right = pltpu.roll(two, (back + 32) % FACE, 1) if (back + 32) % FACE else two
        moved.append(jnp.where(lane < 32, left[:, :128], right[:, :128]))
    parts = [moved[group % 8][8 * (group // 8) : 8 * (group // 8) + 8, :] for group in range(GROUPS)]
    return jnp.concatenate(parts, axis=0)


def pack(table, sends, first, second, third, fourth):
    first[:ROWS, :] = pick(table, sends[0:1, :])
    first[ROWS:, :] = fold(pick(table, sends[4:5, :]))
    second[:ROWS, :] = pick(table, sends[1:2, :])
    second[ROWS:, :] = fold(pick(table, sends[5:6, :]))
    third[...] = pick(table, sends[2:3, :])
    fourth[...] = pick(table, sends[3:4, :])


def bonds_into(total, table, index, inside, tangent, position, stiffness, rest_length, intact, owned):
    count = position.shape[1]
    tang = tangent.shape[1]
    slot = lax.broadcasted_iota(jnp.int32, (1, count), 1)
    live = slot < owned
    own = [tangent[c] for c in range(3)]
    force = [total[3 * tang + c : 3 * tang + c + 1, :] for c in range(3)]
    for bond in range(index.shape[0]):
        rows = pick(table, index[bond : bond + 1, :])
        weight = jnp.where(live & inside[bond : bond + 1, :], intact[bond : bond + 1, :].astype(jnp.float32), 0.0)
        stiff = stiffness[bond : bond + 1, :] * weight
        rest = rest_length[bond : bond + 1, :]
        delta = [rows[3 * tang + c : 3 * tang + c + 1, :] - position[c : c + 1, :] for c in range(3)]
        inverse = lax.rsqrt(delta[0] * delta[0] + delta[1] * delta[1] + delta[2] * delta[2] + 0.25)
        scaled = stiff * (1.0 - rest * inverse)
        curved = stiff * rest * (inverse * inverse * inverse)
        dtang = [rows[c * tang : (c + 1) * tang, :] - own[c] for c in range(3)]
        along = delta[0] * dtang[0] + delta[1] * dtang[1] + delta[2] * dtang[2]
        for c in range(3):
            force[c] = force[c] + scaled * delta[c]
            total[c * tang : (c + 1) * tang, :] += scaled * dtang[c] + (curved * delta[c]) * along
    for c in range(3):
        total[3 * tang + c : 3 * tang + c + 1, :] = force[c]


def place_of(index, odd):
    own = index < 512
    face = (index - 512) >> 8
    is_corner = index >= 1536
    corner = (index - 1536) >> 4
    upward = jnp.where(is_corner, corner & 1, (face >> 1) & 1)
    forward = jnp.where(is_corner, corner >> 1, (face >> 1) & 1)
    second_l = jnp.where(forward == odd[0], 1, 0)
    second_h = jnp.where(upward == odd[1], 1, 0)
    on_l = (face == 0) | (face == 3)
    at_face = jnp.where(on_l, 512 + 256 * second_l, 1280 - 256 * second_h) + (index & 255)
    at_corner = 1536 + 32 * second_h + 16 * (second_l ^ second_h) + (index & 15)
    return jnp.where(own, index, jnp.where(is_corner, at_corner, at_face))


def pack_kernel(tangent, position, sends, first, second, third, fourth):
    table = halves(stacked(tangent[...], position[...]))
    pack(table, sends, first, second, third, fourth)


def own_kernel(odd, owned, params, tangent, position, basis, stiffness, rest_length, neighbours, intact, total):
    tang = tangent.shape[1]
    count = position.shape[1]
    for c in range(3):
        total[c * tang : (c + 1) * tang, :] = basis[c]
        outer = jnp.zeros((1, count), jnp.float32)
        for p in range(tang):
            outer = outer + params[p] * basis[c, p : p + 1, :]
        total[3 * tang + c : 3 * tang + c + 1, :] = outer
    total[3 * tang + 3 : ROWS, :] = jnp.zeros((ROWS - 3 * tang - 3, count), jnp.float32)
    table = halves(stacked(tangent[...], position[...]))
    index = neighbours[...]
    inside = index < 512
    bonds_into(total, table, index, inside, tangent, position, stiffness, rest_length, intact, owned[0])


def side_kernel(odd, owned, before, first, second, both, tangent, position, stiffness, rest_length, neighbours, intact, total):
    total[...] = before[...]
    fourth = both.at[1 - odd[1]]
    table = halves(jnp.concatenate([first[:ROWS, :], second[:ROWS, :], fourth[:ROWS, :]], axis=1))
    index = place_of(neighbours[...], odd) - 512
    inside = (index >= 0) & (index < 768)
    bonds_into(total, table, index, inside, tangent, position, stiffness, rest_length, intact, owned[0])


def height_kernel(last):
    def body(odd, owned, before, third, both, tangent, position, tangent_vel, velocity, mass, stiffness, rest_length, neighbours, intact, sends, *outs):
        new_tangent, new_position, new_tangent_vel, new_velocity = outs[:4]
        total = outs[-1]
        tang = tangent.shape[1]
        total[...] = before[...]
        fourth = both.at[1 - odd[1]]
        corners = unfold(third[ROWS:, :], fourth[ROWS:, :])
        table = halves(jnp.concatenate([third[:ROWS, :], corners], axis=1))[:, : FACE + 64]
        index = place_of(neighbours[...], odd) - 1280
        inside = index >= 0
        bonds_into(total, table, index, inside, tangent, position, stiffness, rest_length, intact, owned[0])
        pace = DT / mass[...]
        for c in range(3):
            speed = tangent_vel[c] + pace * total[c * tang : (c + 1) * tang, :]
            new_tangent_vel[c] = speed
            new_tangent[c] = tangent[c] + DT * speed
        speed = velocity[...] + pace * total[3 * tang : 3 * tang + 3, :]
        new_velocity[...] = speed
        new_position[...] = position[...] + DT * speed
        if not last:
            table = halves(stacked(new_tangent[...], new_position[...]))
            pack(table, sends, *outs[4:8])

    return body


def cost(columns, bonds, moved):
    return pl.CostEstimate(flops=2 * 2 * ROWS * columns * bonds * 512, bytes_accessed=moved, transcendentals=0)


def f32(*shape):
    return jax.ShapeDtypeStruct(shape, jnp.float32)


VMEM = pl.BlockSpec(memory_space=pltpu.VMEM)
SMEM = pl.BlockSpec(memory_space=pltpu.SMEM)


def on_device(
    position,
    velocity,
    tangent_pos,
    tangent_vel,
    mass,
    load_basis,
    params,
    stiffness,
    rest_length,
    neighbours,
    intact,
    face_lists,
    corner_lists,
    owned,
):
    count = position.shape[1]
    bonds = neighbours.shape[0]
    strips, levels = lax.axis_size("len"), lax.axis_size("height")
    odd_l = lax.axis_index("len") % 2
    odd_h = lax.axis_index("height") % 2
    odd = jnp.stack([odd_l, odd_h]).astype(jnp.int32)
    mass = mass.reshape(1, count)

    def either(flag, yes, no):
        return jnp.where(flag == 1, yes, no)

    up = [either(odd_h, corner_lists[2 * a + 1], corner_lists[2 * a]) for a in range(2)]
    down = [either(odd_h, corner_lists[2 * a], corner_lists[2 * a + 1]) for a in range(2)]
    sends = jnp.stack(
        [
            either(odd_l, face_lists[3], face_lists[0]),
            either(odd_l, face_lists[0], face_lists[3]),
            either(odd_h, face_lists[2], face_lists[1]),
            either(odd_h, face_lists[1], face_lists[2]),
            jnp.tile(jnp.concatenate([either(odd_l, up[1], up[0]), either(odd_l, down[1], down[0])]), 8),
            jnp.tile(jnp.concatenate([either(odd_l, down[0], down[1]), either(odd_l, up[0], up[1])]), 8),
        ]
    )
    low = lax.broadcasted_iota(jnp.int32, (MESSAGE - ROWS, FACE), 1) % 32 < CORNER
    packed = (f32(MESSAGE, FACE), f32(MESSAGE, FACE), f32(ROWS, FACE), f32(ROWS, FACE))
    messages = pl.pallas_call(
        pack_kernel,
        out_shape=packed,
        compiler_params=PARAMS,
        cost_estimate=cost(512, 3, 700000),
        name="pack",
    )(tangent_pos, position, sends)
    for step in range(STEPS):
        last = step == STEPS - 1
        first = lax.ppermute(messages[0], AXES, matching(strips, levels, 0, 1))
        second = lax.ppermute(messages[1], AXES, matching(strips, levels, 0, 0))
        total = pl.pallas_call(
            own_kernel,
            out_shape=f32(ROWS, count),
            in_specs=[SMEM] * 3 + [VMEM] * 7,
            compiler_params=PARAMS,
            cost_estimate=cost(512, bonds, 1000000),
            name="own_bonds",
        )(odd, owned, params, tangent_pos, position, load_basis, stiffness, rest_length, neighbours, intact)
        first, second, total = lax.optimization_barrier((first, second, total))
        mine = jnp.where(low, second[ROWS:], first[ROWS:])
        beside = jnp.concatenate([messages[3], mine])
        mine = jnp.where(low, first[ROWS:], second[ROWS:])
        third = lax.ppermute(jnp.concatenate([messages[2], mine]), AXES, matching(strips, levels, 1, 1))
        both = lax.all_gather(beside, AXES, axis_index_groups=couples(strips, levels))
        total = pl.pallas_call(
            side_kernel,
            out_shape=f32(ROWS, count),
            in_specs=[SMEM] * 2 + [VMEM] * 10,
            compiler_params=PARAMS,
            cost_estimate=cost(1, bonds, 1000),
            name="side_bonds",
        )(odd, owned, total, first, second, both, tangent_pos, position, stiffness, rest_length, neighbours, intact)
        state = (f32(*tangent_pos.shape), f32(*position.shape), f32(*tangent_pos.shape), f32(*position.shape))
        out = pl.pallas_call(
            height_kernel(last),
            out_shape=state if last else state + packed,
            in_specs=[SMEM] * 2 + [VMEM] * 13,
            scratch_shapes=[pltpu.VMEM((ROWS, count), jnp.float32)],
            compiler_params=PARAMS,
            cost_estimate=cost(320, bonds, 1500000),
            name="height_bonds",
        )(odd, owned, total, third, both, tangent_pos, position, tangent_vel, velocity, mass, stiffness, rest_length, neighbours, intact, sends)
        tangent_pos, position, tangent_vel, velocity = out[:4]
        messages = out[4:]
    return (position, velocity, tangent_pos, tangent_vel)


def solution(mesh):
    placed = (
        P(None, ("len", "height")),
        P(None, ("len", "height")),
        P(None, None, ("len", "height")),
        P(None, None, ("len", "height")),
        P(("len", "height")),
        P(None, None, ("len", "height")),
        P(),
        P(None, ("len", "height")),
        P(None, ("len", "height")),
        P(None, ("len", "height")),
        P(None, ("len", "height")),
        P(None, ("len", "height")),
        P(None, ("len", "height")),
        P(("len", "height")),
    )
    return jax.shard_map(
        on_device,
        mesh=mesh,
        in_specs=placed,
        out_specs=(
            P(None, ("len", "height")),
            P(None, ("len", "height")),
            P(None, None, ("len", "height")),
            P(None, None, ("len", "height")),
        ),
        check_vma=False,
    )
```

```python
import jax
import jax.numpy as jnp
from jax import lax
from jax.experimental import pallas as pl
from jax.experimental.pallas import tpu as pltpu
from jax.sharding import PartitionSpec as P

STEPS = 2
DT = 0.05
FACE = 256
CORNER = 16
ROWS = 104
MESSAGE = ROWS + 16
GROUPS = ROWS // 8
AXES = ("len", "height")
PARAMS = pltpu.CompilerParams(vmem_limit_bytes=16 * 2**20)


def matching(strips, levels, along, odd):
    pairs = []
    for l in range(strips):
        for h in range(levels):
            place, size = (l, strips) if along == 0 else (h, levels)
            other = place + 1 if place % 2 == odd else place - 1
            if 0 <= other < size:
                pairs.append((l * levels + h, other * levels + h if along == 0 else l * levels + other))
    return pairs


def couples(strips, levels):
    return [[l * levels + h, l * levels + h + 1] for l in range(strips) for h in range(0, levels, 2)]


def halves(table):
    high = table.astype(jnp.bfloat16).astype(jnp.float32)
    return jnp.concatenate([high, table - high], axis=0).astype(jnp.bfloat16)


def one_hot(index, rows):
    lanes = index.shape[1]
    wanted = jnp.broadcast_to(index, (16, lanes)).astype(jnp.int16)
    base = lax.broadcasted_iota(jnp.int16, (16, lanes), 0)
    one = jnp.ones((16, lanes), jnp.bfloat16)
    zero = jnp.zeros((16, lanes), jnp.bfloat16)
    parts = [jnp.where(wanted == base + jnp.int16(first), one, zero) for first in range(0, rows, 16)]
    return jnp.concatenate(parts, axis=0)


def pick(table, index):
    both = jnp.dot(table, one_hot(index, table.shape[1]), preferred_element_type=jnp.float32)
    return both[:ROWS] + both[ROWS:]


def stacked(tangent, position):
    lanes = position.shape[1]
    tang = tangent.shape[0] * tangent.shape[1]
    flat = tangent.reshape(tang, lanes)
    return jnp.concatenate([flat, position, jnp.zeros((ROWS - tang - 3, lanes), jnp.float32)], axis=0)


def fold(columns):
    slot = lax.broadcasted_iota(jnp.int32, (8, FACE), 1) >> 5
    parts = []
    for first in range(0, GROUPS, 8):
        part = jnp.zeros((8, FACE), jnp.float32)
        for group in range(first, min(first + 8, GROUPS)):
            part = jnp.where(slot == group - first, columns[8 * group : 8 * group + 8, :], part)
        parts.append(part)
    return jnp.concatenate(parts, axis=0)


def unfold(one, two):
    lane = lax.broadcasted_iota(jnp.int32, (16, 128), 1)
    moved = []
    for slot in range(8):
        back = (FACE - 32 * slot) % FACE
        left = one if back == 0 else pltpu.roll(one, back, 1)
        right = pltpu.roll(two, (back + 32) % FACE, 1) if (back + 32) % FACE else two
        moved.append(jnp.where(lane < 32, left[:, :128], right[:, :128]))
    parts = [moved[group % 8][8 * (group // 8) : 8 * (group // 8) + 8, :] for group in range(GROUPS)]
    return jnp.concatenate(parts, axis=0)


def pack_len(table, sends, first, second):
    first[:ROWS, :] = pick(table, sends[0:1, :])
    first[ROWS:, :] = fold(pick(table, sends[4:5, :]))
    second[:ROWS, :] = pick(table, sends[1:2, :])
    second[ROWS:, :] = fold(pick(table, sends[5:6, :]))


def bonds_into(total, table, index, inside, tangent, position, stiffness, rest_length, weights):
    tang = tangent.shape[1]
    own = [tangent[c] for c in range(3)]
    force = [total[3 * tang + c : 3 * tang + c + 1, :] for c in range(3)]
    for bond in range(index.shape[0]):
        rows = pick(table, index[bond : bond + 1, :])
        weight = jnp.where(inside[bond : bond + 1, :], weights[bond : bond + 1, :], 0.0)
        stiff = stiffness[bond : bond + 1, :] * weight
        rest = rest_length[bond : bond + 1, :]
        delta = [rows[3 * tang + c : 3 * tang + c + 1, :] - position[c : c + 1, :] for c in range(3)]
        inverse = lax.rsqrt(delta[0] * delta[0] + delta[1] * delta[1] + delta[2] * delta[2] + 0.25)
        scaled = stiff * (1.0 - rest * inverse)
        curved = stiff * rest * (inverse * inverse * inverse)
        dtang = [rows[c * tang : (c + 1) * tang, :] - own[c] for c in range(3)]
        along = delta[0] * dtang[0] + delta[1] * dtang[1] + delta[2] * dtang[2]
        for c in range(3):
            force[c] = force[c] + scaled * delta[c]
            total[c * tang : (c + 1) * tang, :] += scaled * dtang[c] + (curved * delta[c]) * along
    for c in range(3):
        total[3 * tang + c : 3 * tang + c + 1, :] = force[c]


def place_of(index, odd_l, odd_h):
    own = index < 512
    face = (index - 512) >> 8
    is_corner = index >= 1536
    corner = (index - 1536) >> 4
    upward = jnp.where(is_corner, corner & 1, (face >> 1) & 1)
    forward = jnp.where(is_corner, corner >> 1, (face >> 1) & 1)
    second_l = jnp.where(forward == odd_l, 1, 0)
    second_h = jnp.where(upward == odd_h, 1, 0)
    on_l = (face == 0) | (face == 3)
    at_face = jnp.where(on_l, 512 + 256 * second_l, 1280 - 256 * second_h) + (index & 255)
    at_corner = 1536 + 32 * second_h + 16 * (second_l ^ second_h) + (index & 15)
    return jnp.where(own, index, jnp.where(is_corner, at_corner, at_face))


def first_kernel(odd, tangent, position, faces, corners, params, first, second, sends, rates, line):
    rates[...] = params[...]
    odd_l = odd[0:1, :FACE]
    odd_h = odd[1:2, :FACE]
    near_l = odd[0:1, :128]
    near_h = odd[1:2, :128]
    line[...] = jnp.zeros(line.shape, jnp.int32)
    line[0:4, 0:CORNER] = corners[...]
    lane = lax.broadcasted_iota(jnp.int32, (8, 128), 1)
    spread = jnp.take_along_axis(line[...], lane & (CORNER - 1), axis=1, mode="promise_in_bounds")
    low = (lane[0:1, :] & (2 * CORNER - 1)) < CORNER
    rows = [spread[c : c + 1, :] for c in range(4)]
    up = [jnp.where(near_h == 1, rows[2 * a + 1], rows[2 * a]) for a in range(2)]
    down = [jnp.where(near_h == 1, rows[2 * a], rows[2 * a + 1]) for a in range(2)]
    one = jnp.where(low, jnp.where(near_l == 1, up[1], up[0]), jnp.where(near_l == 1, down[1], down[0]))
    two = jnp.where(low, jnp.where(near_l == 1, down[0], down[1]), jnp.where(near_l == 1, up[0], up[1]))
    sends[0:1, :] = jnp.where(odd_l == 1, faces[3:4, :], faces[0:1, :])
    sends[1:2, :] = jnp.where(odd_l == 1, faces[0:1, :], faces[3:4, :])
    sends[2:3, :] = jnp.where(odd_h == 1, faces[2:3, :], faces[1:2, :])
    sends[3:4, :] = jnp.where(odd_h == 1, faces[1:2, :], faces[2:3, :])
    sends[4:5, :] = jnp.concatenate([one, one], axis=1)
    sends[5:6, :] = jnp.concatenate([two, two], axis=1)
    sends[6:8, :] = jnp.zeros((2, FACE), jnp.int32)
    pack_len(halves(stacked(tangent[...], position[...])), sends, first, second)


def own_bonds(params, tangent, position, basis, stiffness, rest_length, index, weights, sends, total, third, fourth):
    tang = tangent.shape[1]
    count = position.shape[1]
    table = halves(stacked(tangent[...], position[...]))
    third[...] = pick(table, sends[2:3, :])
    fourth[...] = pick(table, sends[3:4, :])
    for c in range(3):
        total[c * tang : (c + 1) * tang, :] = basis[c]
        total[3 * tang + c : 3 * tang + c + 1, :] = jnp.dot(params[...], basis[c], precision=lax.Precision.HIGHEST, preferred_element_type=jnp.float32)
    total[3 * tang + 3 : ROWS, :] = jnp.zeros((ROWS - 3 * tang - 3, count), jnp.float32)
    bonds_into(total, table, index, index < 512, tangent, position, stiffness, rest_length, weights)


def own_kernel(odd, owned, params, tangent, position, basis, stiffness, rest_length, neighbours, intact, sends, total, third, fourth, placed, weights):
    index = neighbours[...]
    placed[...] = place_of(index, odd[0:1, :], odd[1:2, :])
    slot = lax.broadcasted_iota(jnp.int32, index.shape, 1)
    weights[...] = jnp.where(slot < owned[...], intact[...].astype(jnp.float32), 0.0)
    own_bonds(params, tangent, position, basis, stiffness, rest_length, index, weights, sends, total, third, fourth)


def own_again_kernel(params, tangent, position, basis, stiffness, rest_length, placed, weights, sends, total, third, fourth):
    own_bonds(params, tangent, position, basis, stiffness, rest_length, placed[...], weights, sends, total, third, fourth)


def partner(both, odd):
    return jnp.where(odd[1:2, :FACE] == 1, both[0], both[1])


def side_kernel(odd, before, first, second, both, tangent, position, stiffness, rest_length, placed, weights, total):
    total[...] = before[...]
    table = halves(jnp.concatenate([first[:ROWS, :], second[:ROWS, :], partner(both, odd)[:ROWS, :]], axis=1))
    index = placed[...] - 512
    inside = (index >= 0) & (index < 768)
    bonds_into(total, table, index, inside, tangent, position, stiffness, rest_length, weights)


def height_kernel(last):
    def body(odd, before, third, both, tangent, position, tangent_vel, velocity, mass, stiffness, rest_length, placed, weights, sends, *outs):
        new_tangent, new_position, new_tangent_vel, new_velocity = outs[:4]
        total = outs[-1]
        tang = tangent.shape[1]
        total[...] = before[...]
        corners = unfold(third[ROWS:, :], partner(both, odd)[ROWS:, :])
        table = halves(jnp.concatenate([third[:ROWS, :], corners], axis=1))[:, : FACE + 64]
        index = placed[...] - 1280
        inside = index >= 0
        bonds_into(total, table, index, inside, tangent, position, stiffness, rest_length, weights)
        pace = DT / mass[...]
        for c in range(3):
            speed = tangent_vel[c] + pace * total[c * tang : (c + 1) * tang, :]
            new_tangent_vel[c] = speed
            new_tangent[c] = tangent[c] + DT * speed
        speed = velocity[...] + pace * total[3 * tang : 3 * tang + 3, :]
        new_velocity[...] = speed
        new_position[...] = position[...] + DT * speed
        if not last:
            table = halves(stacked(new_tangent[...], new_position[...]))
            pack_len(table, sends, *outs[4:6])

    return body


def cost(columns, bonds, moved):
    return pl.CostEstimate(flops=2 * 2 * ROWS * columns * bonds * 512, bytes_accessed=moved, transcendentals=0)


def i32(*shape):
    return jax.ShapeDtypeStruct(shape, jnp.int32)


def f32(*shape):
    return jax.ShapeDtypeStruct(shape, jnp.float32)


def on_device(
    position,
    velocity,
    tangent_pos,
    tangent_vel,
    mass,
    load_basis,
    params,
    stiffness,
    rest_length,
    neighbours,
    intact,
    face_lists,
    corner_lists,
    owned,
):
    count = position.shape[1]
    bonds = neighbours.shape[0]
    strips, levels = lax.axis_size("len"), lax.axis_size("height")
    odd_l = lax.axis_index("len") % 2
    odd_h = lax.axis_index("height") % 2
    odd = jnp.stack([jnp.full((count,), odd_l, jnp.int32), jnp.full((count,), odd_h, jnp.int32)])
    mass = mass.reshape(1, count)

    low = lax.broadcasted_iota(jnp.int32, (MESSAGE - ROWS, FACE), 1) % 32 < CORNER
    packed = (f32(MESSAGE, FACE), f32(MESSAGE, FACE))
    *messages, sends, rates = pl.pallas_call(
        first_kernel,
        out_shape=packed + (i32(8, FACE), f32(1, params.shape[0])),
        scratch_shapes=[pltpu.VMEM((8, 128), jnp.int32)],
        compiler_params=PARAMS,
        cost_estimate=cost(512, 3, 700000),
        name="first_messages",
    )(odd, tangent_pos, position, face_lists, corner_lists, params.reshape(1, -1))
    for step in range(STEPS):
        last = step == STEPS - 1
        first = lax.ppermute(messages[0], AXES, matching(strips, levels, 0, 1))
        second = lax.ppermute(messages[1], AXES, matching(strips, levels, 0, 0))
        made = (f32(ROWS, count), f32(ROWS, FACE), f32(ROWS, FACE))
        if step == 0:
            total, faces_z, faces_core, placed, weights = pl.pallas_call(
                own_kernel,
                out_shape=made + (i32(bonds, count), f32(bonds, count)),
                compiler_params=PARAMS,
                cost_estimate=cost(512, bonds, 1000000),
                name="own_bonds",
            )(odd, owned.reshape(1, 1), rates, tangent_pos, position, load_basis, stiffness, rest_length, neighbours, intact, sends)
        else:
            total, faces_z, faces_core = pl.pallas_call(
                own_again_kernel,
                out_shape=made,
                compiler_params=PARAMS,
                cost_estimate=cost(512, bonds, 1000000),
                name="own_bonds_again",
            )(rates, tangent_pos, position, load_basis, stiffness, rest_length, placed, weights, sends)
        first, second, total = lax.optimization_barrier((first, second, total))
        mine = jnp.where(low, second[ROWS:], first[ROWS:])
        beside = jnp.concatenate([faces_core, mine])
        mine = jnp.where(low, first[ROWS:], second[ROWS:])
        third = lax.ppermute(jnp.concatenate([faces_z, mine]), AXES, matching(strips, levels, 1, 1))
        both = lax.all_gather(beside, AXES, axis_index_groups=couples(strips, levels))
        total = pl.pallas_call(
            side_kernel,
            out_shape=f32(ROWS, count),
            compiler_params=PARAMS,
            cost_estimate=cost(1, bonds, 1000),
            name="side_bonds",
        )(odd, total, first, second, both, tangent_pos, position, stiffness, rest_length, placed, weights)
        state = (f32(*tangent_pos.shape), f32(*position.shape), f32(*tangent_pos.shape), f32(*position.shape))
        out = pl.pallas_call(
            height_kernel(last),
            out_shape=state if last else state + packed,
            scratch_shapes=[pltpu.VMEM((ROWS, count), jnp.float32)],
            compiler_params=PARAMS,
            cost_estimate=cost(320, bonds, 1500000),
            name="height_bonds",
        )(odd, total, third, both, tangent_pos, position, tangent_vel, velocity, mass, stiffness, rest_length, placed, weights, sends)
        tangent_pos, position, tangent_vel, velocity = out[:4]
        messages = out[4:]
    return (position, velocity, tangent_pos, tangent_vel)


def solution(mesh):
    placed = (
        P(None, ("len", "height")),
        P(None, ("len", "height")),
        P(None, None, ("len", "height")),
        P(None, None, ("len", "height")),
        P(("len", "height")),
        P(None, None, ("len", "height")),
        P(),
        P(None, ("len", "height")),
        P(None, ("len", "height")),
        P(None, ("len", "height")),
        P(None, ("len", "height")),
        P(None, ("len", "height")),
        P(None, ("len", "height")),
        P(("len", "height")),
    )
    return jax.shard_map(
        on_device,
        mesh=mesh,
        in_specs=placed,
        out_specs=(
            P(None, ("len", "height")),
            P(None, ("len", "height")),
            P(None, None, ("len", "height")),
            P(None, None, ("len", "height")),
        ),
        check_vma=False,
    )
```

```python
import jax
import jax.numpy as jnp
from jax import lax
from jax.experimental import pallas as pl
from jax.experimental.pallas import tpu as pltpu
from jax.sharding import PartitionSpec as P

STEPS = 2
DT = 0.05
FACE = 256
CORNER = 16
ROWS = 104
USED = 99
MESSAGE = ROWS + 8
GROUPS = ROWS // 8
AXES = ("len", "height")
PARAMS = pltpu.CompilerParams(vmem_limit_bytes=16 * 2**20)


def matching(strips, levels, along, odd):
    pairs = []
    for l in range(strips):
        for h in range(levels):
            place, size = (l, strips) if along == 0 else (h, levels)
            other = place + 1 if place % 2 == odd else place - 1
            if 0 <= other < size:
                pairs.append((l * levels + h, other * levels + h if along == 0 else l * levels + other))
    return pairs


def couples(strips, levels):
    return [[l * levels + h, l * levels + h + 1] for l in range(strips) for h in range(0, levels, 2)]


def halves(table):
    high = table.astype(jnp.bfloat16).astype(jnp.float32)
    return jnp.concatenate([high, table - high], axis=0).astype(jnp.bfloat16)


def one_hot(index, rows):
    lanes = index.shape[1]
    wanted = jnp.broadcast_to(index, (16, lanes)).astype(jnp.int16)
    base = lax.broadcasted_iota(jnp.int16, (16, lanes), 0)
    one = jnp.ones((16, lanes), jnp.bfloat16)
    zero = jnp.zeros((16, lanes), jnp.bfloat16)
    parts = [jnp.where(wanted == base + jnp.int16(first), one, zero) for first in range(0, rows, 16)]
    return jnp.concatenate(parts, axis=0)


def pick(table, index):
    both = jnp.dot(table, one_hot(index, table.shape[1]), preferred_element_type=jnp.float32)
    return both[:ROWS] + both[ROWS:]


def stacked(tangent, position):
    lanes = position.shape[1]
    tang = tangent.shape[0] * tangent.shape[1]
    flat = tangent.reshape(tang, lanes)
    return jnp.concatenate([flat, position, jnp.zeros((ROWS - tang - 3, lanes), jnp.float32)], axis=0)


def fold(columns, message):
    slot = lax.broadcasted_iota(jnp.int32, (8, FACE), 1) >> 5
    level = lax.broadcasted_iota(jnp.int32, (8, FACE), 0)
    part = jnp.zeros((8, FACE), jnp.float32)
    for group in range(GROUPS):
        block = columns[8 * group : 8 * group + 8, :]
        block = jnp.concatenate([block, block], axis=1)
        if group < 8:
            part = jnp.where(slot == group, block, part)
        else:
            line = jnp.sum(jnp.where(slot == level, block, 0.0), axis=0, keepdims=True)
            message[USED + group - 8 : USED + group - 7, :] = line
    message[ROWS:, :] = part


def raised(line):
    level = lax.broadcasted_iota(jnp.int32, (8, 128), 0)
    wide = jnp.broadcast_to(line, (8, FACE))
    near = jnp.where(level < 4, wide[:, :128], wide[:, 128:])
    rows = near
    for run in range(1, 4):
        rows = jnp.where((level & 3) == run, pltpu.roll(near, 128 - 32 * run, 1), rows)
    return rows


def unfold(one, two):
    lane = lax.broadcasted_iota(jnp.int32, (8, 128), 1)
    parts = []
    for group in range(GROUPS):
        if group < 8:
            back = (FACE - 32 * group) % FACE
            left, right = one[ROWS:, :], two[ROWS:, :]
            left = pltpu.roll(left, back, 1) if back else left
            right = pltpu.roll(right, (back + 32) % FACE, 1) if (back + 32) % FACE else right
        else:
            left, right = [raised(message[USED + group - 8 : USED + group - 7, :]) for message in (one, two)]
            right = pltpu.roll(right, 32, 1)
        parts.append(jnp.where(lane < 32, left[:, :128], right[:, :128]))
    return jnp.concatenate(parts, axis=0)


def pack_len(table, sends, first, second):
    corners = pick(table, jnp.concatenate([sends[4:5, :128], sends[5:6, :128]], axis=1))
    first[:ROWS, :] = pick(table, sends[0:1, :])
    fold(corners[:, :128], first)
    second[:ROWS, :] = pick(table, sends[1:2, :])
    fold(corners[:, 128:], second)


def bonds_into(total, table, index, inside, tangent, position, stiffness, rest_length, weights):
    tang = tangent.shape[1]
    own = [tangent[c] for c in range(3)]
    force = [total[3 * tang + c : 3 * tang + c + 1, :] for c in range(3)]
    for bond in range(index.shape[0]):
        rows = pick(table, index[bond : bond + 1, :])
        weight = jnp.where(inside[bond : bond + 1, :], weights[bond : bond + 1, :], 0.0)
        stiff = stiffness[bond : bond + 1, :] * weight
        rest = rest_length[bond : bond + 1, :]
        delta = [rows[3 * tang + c : 3 * tang + c + 1, :] - position[c : c + 1, :] for c in range(3)]
        inverse = lax.rsqrt(delta[0] * delta[0] + delta[1] * delta[1] + delta[2] * delta[2] + 0.25)
        scaled = stiff * (1.0 - rest * inverse)
        curved = stiff * rest * (inverse * inverse * inverse)
        dtang = [rows[c * tang : (c + 1) * tang, :] - own[c] for c in range(3)]
        along = delta[0] * dtang[0] + delta[1] * dtang[1] + delta[2] * dtang[2]
        for c in range(3):
            force[c] = force[c] + scaled * delta[c]
            total[c * tang : (c + 1) * tang, :] += scaled * dtang[c] + (curved * delta[c]) * along
    for c in range(3):
        total[3 * tang + c : 3 * tang + c + 1, :] = force[c]


def place_of(index, odd_l, odd_h):
    own = index < 512
    face = (index - 512) >> 8
    is_corner = index >= 1536
    corner = (index - 1536) >> 4
    upward = jnp.where(is_corner, corner & 1, (face >> 1) & 1)
    forward = jnp.where(is_corner, corner >> 1, (face >> 1) & 1)
    second_l = jnp.where(forward == odd_l, 1, 0)
    second_h = jnp.where(upward == odd_h, 1, 0)
    on_l = (face == 0) | (face == 3)
    at_face = jnp.where(on_l, 512 + 256 * second_l, 1280 - 256 * second_h) + (index & 255)
    at_corner = 1536 + 32 * second_h + 16 * (second_l ^ second_h) + (index & 15)
    return jnp.where(own, index, jnp.where(is_corner, at_corner, at_face))


def first_kernel(odd, tangent, position, faces, corners, params, first, second, sends, rates, line):
    rates[...] = params[...]
    odd_l = odd[0:1, :FACE]
    odd_h = odd[1:2, :FACE]
    near_l = odd[0:1, :128]
    near_h = odd[1:2, :128]
    line[...] = jnp.zeros(line.shape, jnp.int32)
    line[0:4, 0:CORNER] = corners[...]
    lane = lax.broadcasted_iota(jnp.int32, (8, 128), 1)
    spread = jnp.take_along_axis(line[...], lane & (CORNER - 1), axis=1, mode="promise_in_bounds")
    low = (lane[0:1, :] & (2 * CORNER - 1)) < CORNER
    rows = [spread[c : c + 1, :] for c in range(4)]
    up = [jnp.where(near_h == 1, rows[2 * a + 1], rows[2 * a]) for a in range(2)]
    down = [jnp.where(near_h == 1, rows[2 * a], rows[2 * a + 1]) for a in range(2)]
    one = jnp.where(low, jnp.where(near_l == 1, up[1], up[0]), jnp.where(near_l == 1, down[1], down[0]))
    two = jnp.where(low, jnp.where(near_l == 1, down[0], down[1]), jnp.where(near_l == 1, up[0], up[1]))
    sends[0:1, :] = jnp.where(odd_l == 1, faces[3:4, :], faces[0:1, :])
    sends[1:2, :] = jnp.where(odd_l == 1, faces[0:1, :], faces[3:4, :])
    sends[2:3, :] = jnp.where(odd_h == 1, faces[2:3, :], faces[1:2, :])
    sends[3:4, :] = jnp.where(odd_h == 1, faces[1:2, :], faces[2:3, :])
    sends[4:5, :] = jnp.concatenate([one, one], axis=1)
    sends[5:6, :] = jnp.concatenate([two, two], axis=1)
    sends[6:8, :] = jnp.zeros((2, FACE), jnp.int32)
    pack_len(halves(stacked(tangent[...], position[...])), sends, first, second)


def own_bonds(params, tangent, position, basis, stiffness, rest_length, index, weights, sends, total, third, fourth):
    tang = tangent.shape[1]
    count = position.shape[1]
    table = halves(stacked(tangent[...], position[...]))
    third[...] = pick(table, sends[2:3, :])
    fourth[...] = pick(table, sends[3:4, :])
    for c in range(3):
        total[c * tang : (c + 1) * tang, :] = basis[c]
        total[3 * tang + c : 3 * tang + c + 1, :] = jnp.dot(params[...], basis[c], precision=lax.Precision.HIGHEST, preferred_element_type=jnp.float32)
    total[3 * tang + 3 : ROWS, :] = jnp.zeros((ROWS - 3 * tang - 3, count), jnp.float32)
    bonds_into(total, table, index, index < 512, tangent, position, stiffness, rest_length, weights)


def own_kernel(odd, owned, params, tangent, position, basis, stiffness, rest_length, neighbours, intact, sends, total, third, fourth, placed, weights):
    index = neighbours[...]
    placed[...] = place_of(index, odd[0:1, :], odd[1:2, :])
    slot = lax.broadcasted_iota(jnp.int32, index.shape, 1)
    weights[...] = jnp.where(slot < owned[...], intact[...].astype(jnp.float32), 0.0)
    own_bonds(params, tangent, position, basis, stiffness, rest_length, index, weights, sends, total, third, fourth)


def own_again_kernel(params, tangent, position, basis, stiffness, rest_length, placed, weights, sends, total, third, fourth):
    own_bonds(params, tangent, position, basis, stiffness, rest_length, placed[...], weights, sends, total, third, fourth)


def partner(both, odd):
    return jnp.where(odd[1:2, :FACE] == 1, both[0], both[1])


def side_kernel(odd, before, first, second, both, tangent, position, stiffness, rest_length, placed, weights, total):
    total[...] = before[...]
    table = halves(jnp.concatenate([first[:ROWS, :], second[:ROWS, :], partner(both, odd)[:ROWS, :]], axis=1))
    index = placed[...] - 512
    inside = (index >= 0) & (index < 768)
    bonds_into(total, table, index, inside, tangent, position, stiffness, rest_length, weights)


def height_kernel(last):
    def body(odd, before, third, both, tangent, position, tangent_vel, velocity, mass, stiffness, rest_length, placed, weights, sends, *outs):
        new_tangent, new_position, new_tangent_vel, new_velocity = outs[:4]
        total = outs[-1]
        tang = tangent.shape[1]
        total[...] = before[...]
        corners = unfold(third[...], partner(both, odd))
        table = halves(jnp.concatenate([third[:ROWS, :], corners], axis=1))[:, : FACE + 64]
        index = placed[...] - 1280
        inside = index >= 0
        bonds_into(total, table, index, inside, tangent, position, stiffness, rest_length, weights)
        pace = DT / mass[...]
        for c in range(3):
            speed = tangent_vel[c] + pace * total[c * tang : (c + 1) * tang, :]
            new_tangent_vel[c] = speed
            new_tangent[c] = tangent[c] + DT * speed
        speed = velocity[...] + pace * total[3 * tang : 3 * tang + 3, :]
        new_velocity[...] = speed
        new_position[...] = position[...] + DT * speed
        if not last:
            table = halves(stacked(new_tangent[...], new_position[...]))
            pack_len(table, sends, *outs[4:6])

    return body


def cost(columns, bonds, moved):
    return pl.CostEstimate(flops=2 * 2 * ROWS * columns * bonds * 512, bytes_accessed=moved, transcendentals=0)


def i32(*shape):
    return jax.ShapeDtypeStruct(shape, jnp.int32)


def f32(*shape):
    return jax.ShapeDtypeStruct(shape, jnp.float32)


def on_device(
    position,
    velocity,
    tangent_pos,
    tangent_vel,
    mass,
    load_basis,
    params,
    stiffness,
    rest_length,
    neighbours,
    intact,
    face_lists,
    corner_lists,
    owned,
):
    count = position.shape[1]
    bonds = neighbours.shape[0]
    strips, levels = lax.axis_size("len"), lax.axis_size("height")
    odd_l = lax.axis_index("len") % 2
    odd_h = lax.axis_index("height") % 2
    odd = jnp.stack([jnp.full((count,), odd_l, jnp.int32), jnp.full((count,), odd_h, jnp.int32)])
    mass = mass.reshape(1, count)

    low = lax.broadcasted_iota(jnp.int32, (MESSAGE - USED, FACE), 1) % 32 < CORNER
    packed = (f32(MESSAGE, FACE), f32(MESSAGE, FACE))
    *messages, sends, rates = pl.pallas_call(
        first_kernel,
        out_shape=packed + (i32(8, FACE), f32(1, params.shape[0])),
        scratch_shapes=[pltpu.VMEM((8, 128), jnp.int32)],
        compiler_params=PARAMS,
        cost_estimate=cost(512, 3, 700000),
        name="first_messages",
    )(odd, tangent_pos, position, face_lists, corner_lists, params.reshape(1, -1))
    for step in range(STEPS):
        last = step == STEPS - 1
        first = lax.ppermute(messages[0], AXES, matching(strips, levels, 0, 1))
        second = lax.ppermute(messages[1], AXES, matching(strips, levels, 0, 0))
        made = (f32(ROWS, count), f32(ROWS, FACE), f32(ROWS, FACE))
        if step == 0:
            total, faces_z, faces_core, placed, weights = pl.pallas_call(
                own_kernel,
                out_shape=made + (i32(bonds, count), f32(bonds, count)),
                compiler_params=PARAMS,
                cost_estimate=cost(512, bonds, 1000000),
                name="own_bonds",
            )(odd, owned.reshape(1, 1), rates, tangent_pos, position, load_basis, stiffness, rest_length, neighbours, intact, sends)
        else:
            total, faces_z, faces_core = pl.pallas_call(
                own_again_kernel,
                out_shape=made,
                compiler_params=PARAMS,
                cost_estimate=cost(512, bonds, 1000000),
                name="own_bonds_again",
            )(rates, tangent_pos, position, load_basis, stiffness, rest_length, placed, weights, sends)
        first, second, total = lax.optimization_barrier((first, second, total))
        mine = jnp.where(low, second[USED:], first[USED:])
        beside = jnp.concatenate([faces_core[:USED], mine])
        mine = jnp.where(low, first[USED:], second[USED:])
        third = lax.ppermute(jnp.concatenate([faces_z[:USED], mine]), AXES, matching(strips, levels, 1, 1))
        both = lax.all_gather(beside, AXES, axis_index_groups=couples(strips, levels))
        total = pl.pallas_call(
            side_kernel,
            out_shape=f32(ROWS, count),
            compiler_params=PARAMS,
            cost_estimate=cost(1, bonds, 1000),
            name="side_bonds",
        )(odd, total, first, second, both, tangent_pos, position, stiffness, rest_length, placed, weights)
        state = (f32(*tangent_pos.shape), f32(*position.shape), f32(*tangent_pos.shape), f32(*position.shape))
        out = pl.pallas_call(
            height_kernel(last),
            out_shape=state if last else state + packed,
            scratch_shapes=[pltpu.VMEM((ROWS, count), jnp.float32)],
            compiler_params=PARAMS,
            cost_estimate=cost(320, bonds, 1500000),
            name="height_bonds",
        )(odd, total, third, both, tangent_pos, position, tangent_vel, velocity, mass, stiffness, rest_length, placed, weights, sends)
        tangent_pos, position, tangent_vel, velocity = out[:4]
        messages = out[4:]
    return (position, velocity, tangent_pos, tangent_vel)


def solution(mesh):
    placed = (
        P(None, ("len", "height")),
        P(None, ("len", "height")),
        P(None, None, ("len", "height")),
        P(None, None, ("len", "height")),
        P(("len", "height")),
        P(None, None, ("len", "height")),
        P(),
        P(None, ("len", "height")),
        P(None, ("len", "height")),
        P(None, ("len", "height")),
        P(None, ("len", "height")),
        P(None, ("len", "height")),
        P(None, ("len", "height")),
        P(("len", "height")),
    )
    return jax.shard_map(
        on_device,
        mesh=mesh,
        in_specs=placed,
        out_specs=(
            P(None, ("len", "height")),
            P(None, ("len", "height")),
            P(None, None, ("len", "height")),
            P(None, None, ("len", "height")),
        ),
        check_vma=False,
    )
```

```python
import jax
import jax.numpy as jnp
from jax import lax
from jax.experimental import pallas as pl
from jax.experimental.pallas import tpu as pltpu
from jax.sharding import PartitionSpec as P

STEPS = 2
DT = 0.05
FACE = 256
CORNER = 16
ROWS = 104
USED = 99
MESSAGE = ROWS + 8
GROUPS = ROWS // 8
AXES = ("len", "height")
PARAMS = pltpu.CompilerParams(vmem_limit_bytes=16 * 2**20)


def matching(strips, levels, along, odd):
    pairs = []
    for l in range(strips):
        for h in range(levels):
            place, size = (l, strips) if along == 0 else (h, levels)
            other = place + 1 if place % 2 == odd else place - 1
            if 0 <= other < size:
                pairs.append((l * levels + h, other * levels + h if along == 0 else l * levels + other))
    return pairs


def couples(strips, levels):
    return [[l * levels + h, l * levels + h + 1] for l in range(strips) for h in range(0, levels, 2)]


def halves(table):
    high = table.astype(jnp.bfloat16).astype(jnp.float32)
    return jnp.concatenate([high, table - high], axis=0).astype(jnp.bfloat16)


def one_hot(index, rows):
    lanes = index.shape[1]
    wanted = jnp.broadcast_to(index, (16, lanes)).astype(jnp.int16)
    base = lax.broadcasted_iota(jnp.int16, (16, lanes), 0)
    one = jnp.ones((16, lanes), jnp.bfloat16)
    zero = jnp.zeros((16, lanes), jnp.bfloat16)
    parts = [jnp.where(wanted == base + jnp.int16(first), one, zero) for first in range(0, rows, 16)]
    return jnp.concatenate(parts, axis=0)


def pick(table, index):
    both = jnp.dot(table, one_hot(index, table.shape[1]), preferred_element_type=jnp.float32)
    return both[:ROWS] + both[ROWS:]


def stacked(tangent, position):
    lanes = position.shape[1]
    tang = tangent.shape[0] * tangent.shape[1]
    flat = tangent.reshape(tang, lanes)
    return jnp.concatenate([flat, position, jnp.zeros((ROWS - tang - 3, lanes), jnp.float32)], axis=0)


def fold(columns, message):
    slot = lax.broadcasted_iota(jnp.int32, (8, FACE), 1) >> 5
    level = lax.broadcasted_iota(jnp.int32, (8, FACE), 0)
    part = jnp.zeros((8, FACE), jnp.float32)
    for group in range(GROUPS):
        block = columns[8 * group : 8 * group + 8, :]
        block = jnp.concatenate([block, block], axis=1)
        if group < 8:
            part = jnp.where(slot == group, block, part)
        else:
            line = jnp.sum(jnp.where(slot == level, block, 0.0), axis=0, keepdims=True)
            message[USED + group - 8 : USED + group - 7, :] = line
    message[ROWS:, :] = part


def raised(line):
    level = lax.broadcasted_iota(jnp.int32, (8, 128), 0)
    wide = jnp.broadcast_to(line, (8, FACE))
    near = jnp.where(level < 4, wide[:, :128], wide[:, 128:])
    rows = near
    for run in range(1, 4):
        rows = jnp.where((level & 3) == run, pltpu.roll(near, 128 - 32 * run, 1), rows)
    return rows


def unfold(one, two):
    lane = lax.broadcasted_iota(jnp.int32, (8, 128), 1)
    parts = []
    for group in range(GROUPS):
        if group < 8:
            back = (FACE - 32 * group) % FACE
            left, right = one[ROWS:, :], two[ROWS:, :]
            left = pltpu.roll(left, back, 1) if back else left
            right = pltpu.roll(right, (back + 32) % FACE, 1) if (back + 32) % FACE else right
        else:
            left, right = [raised(message[USED + group - 8 : USED + group - 7, :]) for message in (one, two)]
            right = pltpu.roll(right, 32, 1)
        parts.append(jnp.where(lane < 32, left[:, :128], right[:, :128]))
    return jnp.concatenate(parts, axis=0)


def pack_len(table, sends, first, second):
    corners = pick(table, jnp.concatenate([sends[4:5, :128], sends[5:6, :128]], axis=1))
    first[:ROWS, :] = pick(table, sends[0:1, :])
    fold(corners[:, :128], first)
    second[:ROWS, :] = pick(table, sends[1:2, :])
    fold(corners[:, 128:], second)


def bonds_into(total, table, index, inside, tangent, position, stiffness, rest_length, weights):
    tang = tangent.shape[1]
    own = [tangent[c] for c in range(3)]
    force = [total[3 * tang + c : 3 * tang + c + 1, :] for c in range(3)]
    for bond in range(index.shape[0]):
        rows = pick(table, index[bond : bond + 1, :])
        weight = jnp.where(inside[bond : bond + 1, :], weights[bond : bond + 1, :], 0.0)
        stiff = stiffness[bond : bond + 1, :] * weight
        rest = rest_length[bond : bond + 1, :]
        delta = [rows[3 * tang + c : 3 * tang + c + 1, :] - position[c : c + 1, :] for c in range(3)]
        inverse = lax.rsqrt(delta[0] * delta[0] + delta[1] * delta[1] + delta[2] * delta[2] + 0.25)
        scaled = stiff * (1.0 - rest * inverse)
        curved = stiff * rest * (inverse * inverse * inverse)
        dtang = [rows[c * tang : (c + 1) * tang, :] - own[c] for c in range(3)]
        along = delta[0] * dtang[0] + delta[1] * dtang[1] + delta[2] * dtang[2]
        for c in range(3):
            force[c] = force[c] + scaled * delta[c]
            total[c * tang : (c + 1) * tang, :] += scaled * dtang[c] + (curved * delta[c]) * along
    for c in range(3):
        total[3 * tang + c : 3 * tang + c + 1, :] = force[c]


def place_of(index, odd_l, odd_h):
    own = index < 512
    face = (index - 512) >> 8
    is_corner = index >= 1536
    corner = (index - 1536) >> 4
    upward = jnp.where(is_corner, corner & 1, (face >> 1) & 1)
    forward = jnp.where(is_corner, corner >> 1, (face >> 1) & 1)
    second_l = jnp.where(forward == odd_l, 1, 0)
    second_h = jnp.where(upward == odd_h, 1, 0)
    on_l = (face == 0) | (face == 3)
    at_face = jnp.where(on_l, 512 + 256 * second_l, 1280 - 256 * second_h) + (index & 255)
    at_corner = 1536 + 32 * second_h + 16 * (second_l ^ second_h) + (index & 15)
    return jnp.where(own, index, jnp.where(is_corner, at_corner, at_face))


def first_kernel(odd, tangent, position, faces, corners, params, first, second, sends, rates, line):
    rates[...] = params[...]
    odd_l = odd[0:1, :FACE]
    odd_h = odd[1:2, :FACE]
    near_l = odd[0:1, :128]
    near_h = odd[1:2, :128]
    line[...] = jnp.zeros(line.shape, jnp.int32)
    line[0:4, 0:CORNER] = corners[...]
    lane = lax.broadcasted_iota(jnp.int32, (8, 128), 1)
    spread = jnp.take_along_axis(line[...], lane & (CORNER - 1), axis=1, mode="promise_in_bounds")
    low = (lane[0:1, :] & (2 * CORNER - 1)) < CORNER
    rows = [spread[c : c + 1, :] for c in range(4)]
    up = [jnp.where(near_h == 1, rows[2 * a + 1], rows[2 * a]) for a in range(2)]
    down = [jnp.where(near_h == 1, rows[2 * a], rows[2 * a + 1]) for a in range(2)]
    one = jnp.where(low, jnp.where(near_l == 1, up[1], up[0]), jnp.where(near_l == 1, down[1], down[0]))
    two = jnp.where(low, jnp.where(near_l == 1, down[0], down[1]), jnp.where(near_l == 1, up[0], up[1]))
    sends[0:1, :] = jnp.where(odd_l == 1, faces[3:4, :], faces[0:1, :])
    sends[1:2, :] = jnp.where(odd_l == 1, faces[0:1, :], faces[3:4, :])
    sends[2:3, :] = jnp.where(odd_h == 1, faces[2:3, :], faces[1:2, :])
    sends[3:4, :] = jnp.where(odd_h == 1, faces[1:2, :], faces[2:3, :])
    sends[4:5, :] = jnp.concatenate([one, one], axis=1)
    sends[5:6, :] = jnp.concatenate([two, two], axis=1)
    sends[6:8, :] = jnp.zeros((2, FACE), jnp.int32)
    pack_len(halves(stacked(tangent[...], position[...])), sends, first, second)


def own_bonds(params, tangent, position, basis, stiffness, rest_length, index, weights, sends, total, third, fourth):
    tang = tangent.shape[1]
    count = position.shape[1]
    table = halves(stacked(tangent[...], position[...]))
    third[...] = pick(table, sends[2:3, :])
    fourth[...] = pick(table, sends[3:4, :])
    for c in range(3):
        total[c * tang : (c + 1) * tang, :] = basis[c]
        total[3 * tang + c : 3 * tang + c + 1, :] = jnp.dot(params[...], basis[c], precision=lax.Precision.HIGHEST, preferred_element_type=jnp.float32)
    total[3 * tang + 3 : ROWS, :] = jnp.zeros((ROWS - 3 * tang - 3, count), jnp.float32)
    bonds_into(total, table, index, index < 512, tangent, position, stiffness, rest_length, weights)


def own_kernel(odd, owned, params, tangent, position, basis, stiffness, rest_length, neighbours, intact, sends, total, third, fourth, placed, weights):
    index = neighbours[...]
    placed[...] = place_of(index, odd[0:1, :], odd[1:2, :])
    slot = lax.broadcasted_iota(jnp.int32, index.shape, 1)
    weights[...] = jnp.where(slot < owned[...], intact[...].astype(jnp.float32), 0.0)
    own_bonds(params, tangent, position, basis, stiffness, rest_length, index, weights, sends, total, third, fourth)


def own_again_kernel(params, tangent, position, basis, stiffness, rest_length, placed, weights, sends, total, third, fourth):
    own_bonds(params, tangent, position, basis, stiffness, rest_length, placed[...], weights, sends, total, third, fourth)


def partner(both, odd):
    return jnp.where(odd[1:2, :FACE] == 1, both[0], both[1])


def side_kernel(odd, before, first, second, both, tangent, position, stiffness, rest_length, placed, weights, total):
    total[...] = before[...]
    table = halves(jnp.concatenate([first[:ROWS, :], second[:ROWS, :], partner(both, odd)[:ROWS, :]], axis=1))
    index = placed[...] - 512
    inside = (index >= 0) & (index < 768)
    bonds_into(total, table, index, inside, tangent, position, stiffness, rest_length, weights)


def height_kernel(last):
    def body(odd, before, third, both, tangent, position, tangent_vel, velocity, mass, stiffness, rest_length, placed, weights, sends, *outs):
        if last:
            far, near = outs[:4], outs[4:8]
            total, sems = outs[8:]
        else:
            near, total = outs[:4], outs[-1]
        new_tangent, new_position, new_tangent_vel, new_velocity = near
        copies = []

        def send(which, *part):
            if last:
                copies.append(pltpu.make_async_copy(near[which].at[part] if part else near[which], far[which].at[part] if part else far[which], sems.at[len(copies)]))
                copies[-1].start()

        tang = tangent.shape[1]
        total[...] = before[...]
        corners = unfold(third[...], partner(both, odd))
        table = halves(jnp.concatenate([third[:ROWS, :], corners], axis=1))[:, : FACE + 64]
        index = placed[...] - 1280
        inside = index >= 0
        bonds_into(total, table, index, inside, tangent, position, stiffness, rest_length, weights)
        pace = DT / mass[...]
        for c in range(3):
            speed = tangent_vel[c] + pace * total[c * tang : (c + 1) * tang, :]
            new_tangent_vel[c] = speed
            send(2, c)
            new_tangent[c] = tangent[c] + DT * speed
            send(0, c)
        speed = velocity[...] + pace * total[3 * tang : 3 * tang + 3, :]
        new_velocity[...] = speed
        send(3)
        new_position[...] = position[...] + DT * speed
        send(1)
        for copy in copies:
            copy.wait()
        if not last:
            table = halves(stacked(new_tangent[...], new_position[...]))
            pack_len(table, sends, *outs[4:6])

    return body


def cost(columns, bonds, moved):
    return pl.CostEstimate(flops=2 * 2 * ROWS * columns * bonds * 512, bytes_accessed=moved, transcendentals=0)


def i32(*shape):
    return jax.ShapeDtypeStruct(shape, jnp.int32)


def f32(*shape):
    return jax.ShapeDtypeStruct(shape, jnp.float32)


def on_device(
    position,
    velocity,
    tangent_pos,
    tangent_vel,
    mass,
    load_basis,
    params,
    stiffness,
    rest_length,
    neighbours,
    intact,
    face_lists,
    corner_lists,
    owned,
):
    count = position.shape[1]
    bonds = neighbours.shape[0]
    strips, levels = lax.axis_size("len"), lax.axis_size("height")
    odd_l = lax.axis_index("len") % 2
    odd_h = lax.axis_index("height") % 2
    odd = jnp.stack([jnp.full((count,), odd_l, jnp.int32), jnp.full((count,), odd_h, jnp.int32)])
    mass = mass.reshape(1, count)

    low = lax.broadcasted_iota(jnp.int32, (MESSAGE - USED, FACE), 1) % 32 < CORNER
    packed = (f32(MESSAGE, FACE), f32(MESSAGE, FACE))
    *messages, sends, rates = pl.pallas_call(
        first_kernel,
        out_shape=packed + (i32(8, FACE), f32(1, params.shape[0])),
        scratch_shapes=[pltpu.VMEM((8, 128), jnp.int32)],
        compiler_params=PARAMS,
        cost_estimate=cost(512, 3, 700000),
        name="first_messages",
    )(odd, tangent_pos, position, face_lists, corner_lists, params.reshape(1, -1))
    for step in range(STEPS):
        last = step == STEPS - 1
        first = lax.ppermute(messages[0], AXES, matching(strips, levels, 0, 1))
        second = lax.ppermute(messages[1], AXES, matching(strips, levels, 0, 0))
        made = (f32(ROWS, count), f32(ROWS, FACE), f32(ROWS, FACE))
        if step == 0:
            total, faces_z, faces_core, placed, weights = pl.pallas_call(
                own_kernel,
                out_shape=made + (i32(bonds, count), f32(bonds, count)),
                compiler_params=PARAMS,
                cost_estimate=cost(512, bonds, 1000000),
                name="own_bonds",
            )(odd, owned.reshape(1, 1), rates, tangent_pos, position, load_basis, stiffness, rest_length, neighbours, intact, sends)
        else:
            total, faces_z, faces_core = pl.pallas_call(
                own_again_kernel,
                out_shape=made,
                compiler_params=PARAMS,
                cost_estimate=cost(512, bonds, 1000000),
                name="own_bonds_again",
            )(rates, tangent_pos, position, load_basis, stiffness, rest_length, placed, weights, sends)
        first, second, total = lax.optimization_barrier((first, second, total))
        mine = jnp.where(low, second[USED:], first[USED:])
        beside = jnp.concatenate([faces_core[:USED], mine])
        mine = jnp.where(low, first[USED:], second[USED:])
        third = lax.ppermute(jnp.concatenate([faces_z[:USED], mine]), AXES, matching(strips, levels, 1, 1))
        both = lax.all_gather(beside, AXES, axis_index_groups=couples(strips, levels))
        total = pl.pallas_call(
            side_kernel,
            out_shape=f32(ROWS, count),
            compiler_params=PARAMS,
            cost_estimate=cost(1, bonds, 1000),
            name="side_bonds",
        )(odd, total, first, second, both, tangent_pos, position, stiffness, rest_length, placed, weights)
        state = (f32(*tangent_pos.shape), f32(*position.shape), f32(*tangent_pos.shape), f32(*position.shape))
        out = pl.pallas_call(
            height_kernel(last),
            out_shape=state if last else state + packed,
            **({"out_specs": [pl.BlockSpec(memory_space=pl.ANY)] * 4} if last else {}),
            scratch_shapes=[pltpu.VMEM(one.shape, one.dtype) for one in state if last]
            + [pltpu.VMEM((ROWS, count), jnp.float32)]
            + [pltpu.SemaphoreType.DMA((8,)) for _ in range(last)],
            compiler_params=PARAMS,
            cost_estimate=cost(320, bonds, 1500000),
            name="height_bonds",
        )(odd, total, third, both, tangent_pos, position, tangent_vel, velocity, mass, stiffness, rest_length, placed, weights, sends)
        tangent_pos, position, tangent_vel, velocity = out[:4]
        messages = out[4:]
    return (position, velocity, tangent_pos, tangent_vel)


def solution(mesh):
    placed = (
        P(None, ("len", "height")),
        P(None, ("len", "height")),
        P(None, None, ("len", "height")),
        P(None, None, ("len", "height")),
        P(("len", "height")),
        P(None, None, ("len", "height")),
        P(),
        P(None, ("len", "height")),
        P(None, ("len", "height")),
        P(None, ("len", "height")),
        P(None, ("len", "height")),
        P(None, ("len", "height")),
        P(None, ("len", "height")),
        P(("len", "height")),
    )
    return jax.shard_map(
        on_device,
        mesh=mesh,
        in_specs=placed,
        out_specs=(
            P(None, ("len", "height")),
            P(None, ("len", "height")),
            P(None, None, ("len", "height")),
            P(None, None, ("len", "height")),
        ),
        check_vma=False,
    )
```
